32 devices in a mesh: dp: 16 (over z, x, core), tensor: 2 (over y).
Axes of the slice: x: 2, y: 2, z: 4, core: 2. Of those that a mesh axis runs over, the one named last changes fastest.
Arguments:
- tokens: bfloat16 [16384, 1024], P(('dp', 'tensor')), may hold values from -6 to 6
- segments: int32 [32, 512], P('dp'), may hold values from 0 to 4, never falling along the last dimension, each value on 1 to 200 neighbouring positions
- w_qkv: bfloat16 [3, 1024, 1024], P(None, 'dp', 'tensor'), may hold values from -0.1875 to 0.1875
- bias_qv: float32 [2, 1024], replicated, may hold values from -3 to 3
- w_out: bfloat16 [1024, 1024], P('tensor', 'dp'), may hold values from -1.5 to 1.5
- bias_out: float32 [1024], replicated, may hold values from -3 to 3
- ln1_gain: float32 [1024], replicated, may hold values from 0.5 to 1.5
- ln1_bias: float32 [1024], replicated, may hold values from -2 to 2
- w_up: bfloat16 [1024, 4096], P('dp', 'tensor'), may hold values from -0.1875 to 0.1875
- bias_up: float32 [4096], replicated, may hold values from -3 to 3
- w_down: bfloat16 [4096, 1024], P('tensor', 'dp'), may hold values from -0.09375 to 0.09375
- bias_down: float32 [1024], replicated, may hold values from -3 to 3
- ln2_gain: float32 [1024], replicated, may hold values from 0.5 to 1.5
- ln2_bias: float32 [1024], replicated, may hold values from -2 to 2
- d_out: bfloat16 [16384, 1024], P(('dp', 'tensor')), may hold values from -6 to 6
Outputs:
- output: bfloat16 [16384, 1024], P(('dp', 'tensor'))
- grad_tokens: float32 [16384, 1024], P(('dp', 'tensor'))
- grad_w_qkv: float32 [3, 1024, 1024], P(None, 'dp', 'tensor')
- grad_bias_qv: float32 [2, 1024], replicated
- grad_w_out: float32 [1024, 1024], P('tensor', 'dp')
- grad_bias_out: float32 [1024], replicated
- grad_ln1_gain: float32 [1024], replicated
- grad_ln1_bias: float32 [1024], replicated
- grad_w_up: float32 [1024, 4096], P('dp', 'tensor')
- grad_bias_up: float32 [4096], replicated
- grad_w_down: float32 [4096, 1024], P('tensor', 'dp')
- grad_bias_down: float32 [1024], replicated
- grad_ln2_gain: float32 [1024], replicated
- grad_ln2_bias: float32 [1024], replicated
The draws below stay inside these ranges and needn't reach their ends.
Inputs may be any that keep to these rules, and one draw needn't show every extreme that they name: `segments`: within each sequence of 512 tokens the segment numbers never fall; each segment is one document.
All inputs are finite; a program needn't handle non-finite values.
Results may differ from the reference program's by a relative error of at most 0.02.
Values may be sent and summed in bfloat16 or wider, within the bound.
No kernel may reach another device: no remote copies, remote signals or barrier semaphores. Data moves between devices by JAX's collectives and lax.ppermute only.
A program may use at most 128 MiB of HBM per device.

```python
import math
import jax
import jax.numpy as jnp
import numpy as np
from jax import lax

D = 1024
HEADS = 16
HEAD_DIM = 64
FF = 4096
SEQ = 512
SEQS_GRP = 2
SEQS = 32
TOKENS = 16384
N_DP = 16
N_TENSOR = 2


def block_levels(stream_key, shape, shards, least, largest):
    gain = 1.0
    for axis_at, blocks in shards:
        draws = jax.random.uniform(jax.random.fold_in(jax.random.fold_in(stream_key, 6), axis_at), (blocks,), jnp.float32, least / len(shards), largest / len(shards))
        gain = gain * jnp.repeat(jnp.exp(draws), shape[axis_at] // blocks).reshape((-1,) + (1,) * (len(shape) - 1 - axis_at))
    return gain


def length_profile(number_of, total, bound, skew):
    loads = [(1 << 20) // math.isqrt(grade ** skew) + 1 for grade in range(2, number_of + 1)]
    spare, counts = total - bound - (number_of - 1), [1] * (number_of - 1)
    while spare > 0:
        free = [i for i in range(number_of - 1) if counts[i] < bound]
        whole, remaining = sum([loads[i] for i in free]), spare
        for i in free:
            more = min(bound - counts[i], max(1, remaining * loads[i] // whole), spare)
            counts[i] = counts[i] + more
            spare = spare - more
    return np.array([bound] + counts)


def uneven(key, amount, total, bound, slope):
    if amount == 2:
        one = jax.random.randint(key, (), max(1, total - bound), min(bound, total - 1) + 1)
        return jnp.stack([one, total - one])
    sizes = jnp.asarray(length_profile(amount, total, bound, slope), jnp.int32)
    couples = (amount - 1) // 2
    giver, sink = sizes[1:1 + 2 * couples:2], sizes[2:2 + 2 * couples:2]
    room = jnp.minimum(giver - 1, bound - sink)
    passed = jax.random.randint(jax.random.fold_in(key, 1), (couples,), 0, 1 << 20) % (room + 1)
    sizes = sizes.at[1:1 + 2 * couples:2].set(giver - passed).at[2:2 + 2 * couples:2].set(sink + passed)
    return sizes[jax.random.permutation(jax.random.fold_in(key, 2), amount)]


def scatter_about(rng, shape, scale, most, pieces=(), kind=jnp.bfloat16):
    values = jax.random.normal(rng, shape, jnp.float32) * scale
    if len(pieces) > 0:
        values = block_levels(rng, shape, pieces, -0.22, 0.18) * values
    return jnp.clip(values, min=-most, max=most).astype(kind)


def setup_inputs(seed: int = 0) -> dict:
    streams_of = jax.random.split(jax.random.key(seed), 16)
    tokens = scatter_about(streams_of[0], (TOKENS, D), 1.0, 6.0, ((0, 32),))
    segments = jax.vmap(lambda own: jnp.searchsorted(jnp.cumsum(uneven(own, max(2, SEQ // 100), SEQ, min(200, SEQ - max(2, SEQ // 100) + 1), 0)), jnp.arange(SEQ), side="right"))(jax.random.split(streams_of[1], SEQS)).reshape((SEQS, SEQ)).astype(jnp.int32)
    w_qkv = scatter_about(streams_of[2], (3, D, D), D ** -0.5, 0.1875, ((1, 16), (2, 2)))
    bias_qv = scatter_about(streams_of[3], (2, D), 0.5, 3.0, (), jnp.float32)
    w_out = scatter_about(streams_of[4], (D, D), (max(D // 64, 4)) ** -0.5, 1.5, ((0, 2), (1, 16)))
    bias_out = scatter_about(streams_of[5], (D,), 0.5, 3.0, (), jnp.float32)
    ln1_gain = jnp.clip(1.0 + 0.1 * jax.random.normal(streams_of[6], (D,), jnp.float32), 0.5, 1.5)
    ln1_bias = scatter_about(streams_of[7], (D,), 0.3, 2.0, (), jnp.float32)
    w_up = scatter_about(streams_of[8], (D, FF), D ** -0.5, 0.1875, ((0, 16), (1, 2)))
    bias_up = scatter_about(streams_of[9], (FF,), 0.5, 3.0, (), jnp.float32)
    w_down = scatter_about(streams_of[10], (FF, D), FF ** -0.5, 0.09375, ((0, 2), (1, 16)))
    bias_down = scatter_about(streams_of[11], (D,), 0.5, 3.0, (), jnp.float32)
    ln2_gain = jnp.clip(1.0 + 0.1 * jax.random.normal(streams_of[12], (D,), jnp.float32), 0.5, 1.5)
    ln2_bias = scatter_about(streams_of[13], (D,), 0.3, 2.0, (), jnp.float32)
    d_out = scatter_about(streams_of[14], (TOKENS, D), 1.0, 6.0, ((0, 32),))
    return {"tokens": tokens, "segments": segments, "w_qkv": w_qkv, "bias_qv": bias_qv, "w_out": w_out, "bias_out": bias_out, "ln1_gain": ln1_gain, "ln1_bias": ln1_bias, "w_up": w_up, "bias_up": bias_up, "w_down": w_down, "bias_down": bias_down, "ln2_gain": ln2_gain, "ln2_bias": ln2_bias, "d_out": d_out}


eps = 1e-12
highest = lax.Precision.HIGHEST

@jax.custom_vjp
def low(v):
    return lax.optimization_barrier(v.astype(jnp.bfloat16)).astype(jnp.float32)

@jax.custom_vjp
def low_back(v):
    return v

def low_keep(v):
    return (low(v), None)

def low_pass(kept, grad):
    return (grad,)

def back_keep(v):
    return (v, None)

def back_low(kept, grad):
    return (low(grad),)
low.defvjp(low_keep, low_pass)
low_back.defvjp(back_keep, back_low)

def layer_norm(inputs, gain_vec, offset):
    center = lax.optimization_barrier(jnp.mean(inputs, axis=-1, keepdims=True))
    spread = lax.rsqrt(lax.optimization_barrier(jnp.mean(jnp.square(inputs - center), axis=-1, keepdims=True)) + eps)
    return (inputs - center) * spread * gain_vec + offset

def split_cols(weight, width):
    return weight.reshape(weight.shape[0], N_TENSOR, width).transpose(1, 0, 2)

def group_copies(rows):
    return low_back(jnp.broadcast_to(rows[:, None, :], (rows.shape[0], N_TENSOR, rows.shape[1])))

def attend(block):
    queries, key_rows, value_rows, segment = block
    raw_scores = low_back(jnp.einsum('qhd,khd->hqk', queries, key_rows, precision=highest))
    same_doc = segment[:, None] == segment[None, :]
    scores = jnp.where(same_doc[None], raw_scores * HEAD_DIM ** (-0.5), -1000000000.0)
    row_max = lax.optimization_barrier(jnp.max(scores, axis=-1, keepdims=True))
    exponent = jnp.exp(scores - row_max)
    probabilities = exponent / lax.optimization_barrier(jnp.sum(exponent, axis=-1, keepdims=True))
    return jnp.einsum('hqk,khd->qhd', low(probabilities), value_rows, precision=highest)

def encoder_layer(params, tokens, segments):
    w_qkv, bias_qv, w_out, bias_out, ln1_gain, ln1_bias, w_up, bias_up, w_down, bias_down, ln2_gain, ln2_bias = params
    head_group = D // N_TENSOR
    unit_group = FF // N_TENSOR
    token_copies = group_copies(tokens)

    def project(weight):
        return jnp.einsum('rtd,tdc->rtc', token_copies, split_cols(weight, head_group), precision=highest).reshape(-1, D)
    queries = low(low_back(project(w_qkv[0]) + bias_qv[0]))
    key_rows = low(low_back(project(w_qkv[1])))
    value_rows = low(low_back(project(w_qkv[2]) + bias_qv[1]))
    shape_seq = (segments.shape[0], SEQ, HEADS, HEAD_DIM)
    context = lax.map(jax.checkpoint(attend), (queries.reshape(shape_seq), key_rows.reshape(shape_seq), value_rows.reshape(shape_seq), segments))
    context = low(low_back(context.reshape(-1, D)))
    attn_parts = jnp.einsum('rtc,tcd->rtd', context.reshape(-1, N_TENSOR, head_group), w_out.reshape(N_TENSOR, head_group, D), precision=highest)
    z_one = tokens + low_back(lax.optimization_barrier(jnp.sum(low(attn_parts), axis=1))) + bias_out
    h_one = layer_norm(z_one, ln1_gain, ln1_bias)
    normed_copies = group_copies(low(h_one))
    up_pre = low_back(jnp.einsum('rtd,tdf->rtf', normed_copies, split_cols(w_up, unit_group), precision=highest).reshape(-1, FF) + bias_up)
    activation = low(jax.nn.gelu(up_pre, approximate=False))
    down_parts = jnp.einsum('rtf,tfd->rtd', activation.reshape(-1, N_TENSOR, unit_group), w_down.reshape(N_TENSOR, unit_group, D), precision=highest)
    z_two = h_one + low_back(lax.optimization_barrier(jnp.sum(low(down_parts), axis=1))) + bias_down
    return layer_norm(z_two, ln2_gain, ln2_bias)

def reference(tokens, segments, w_qkv, bias_qv, w_out, bias_out, ln1_gain, ln1_bias, w_up, bias_up, w_down, bias_down, ln2_gain, ln2_bias, d_out):
    params = tuple((item.astype(jnp.float32) for item in (w_qkv, bias_qv, w_out, bias_out, ln1_gain, ln1_bias, w_up, bias_up, w_down, bias_down, ln2_gain, ln2_bias)))
    group_rows = SEQS_GRP * SEQ
    token_groups = tokens.astype(jnp.float32).reshape(N_DP, group_rows, D)
    cotangent_groups = d_out.astype(jnp.float32).reshape(N_DP, group_rows, D)
    segment_groups = segments.reshape(N_DP, SEQS_GRP, SEQ)

    def step(running, block):
        token_block, segment_block, cotangent_block = block

        def forward(weights, inputs):
            return encoder_layer(weights, inputs, segment_block)
        result, pullback = jax.vjp(forward, params, token_block)
        grad_params, grad_inputs = pullback(cotangent_block)
        return (jax.tree.map(jnp.add, running, grad_params), (result.astype(jnp.bfloat16), grad_inputs))
    start = jax.tree.map(jnp.zeros_like, params)
    sums, (outputs, grad_inputs) = lax.scan(step, start, (token_groups, segment_groups, cotangent_groups))
    return (outputs.reshape(TOKENS, D), grad_inputs.reshape(TOKENS, D), sums[0], sums[1], sums[2], sums[3], sums[4], sums[5], sums[6], sums[7], sums[8], sums[9], sums[10], sums[11])
```

```python
import functools

import jax
import jax.numpy as jnp
from jax import lax
from jax.experimental import pallas as pl
from jax.experimental.pallas import tpu as pltpu
from jax.sharding import PartitionSpec as P

HEAD_DIM = 64
SEQ = 512


eps = 1e-12


def matmul(left, right):
    return jnp.dot(left, right, preferred_element_type=jnp.float32)


def inner_rows(left, right):
    return lax.dot_general(
        left, right, (((0,), (0,)), ((), ())), preferred_element_type=jnp.float32
    )


def outer_cols(left, right):
    return lax.dot_general(
        left, right, (((1,), (1,)), ((), ())), preferred_element_type=jnp.float32
    )


def norm_forward(inputs, gain_vec, offset):
    center = jnp.mean(inputs, axis=-1, keepdims=True)
    spread = lax.rsqrt(jnp.mean(jnp.square(inputs - center), axis=-1, keepdims=True) + eps)
    scaled = (inputs - center) * spread
    return (scaled * gain_vec + offset, scaled, spread)


def norm_backward(gradient, scaled, spread, gain_vec):
    d_gain = jnp.sum(gradient * scaled, axis=0)
    d_offset = jnp.sum(gradient, axis=0)
    d_scaled = gradient * gain_vec
    d_inputs = spread * (
        d_scaled
        - jnp.mean(d_scaled, axis=-1, keepdims=True)
        - scaled * jnp.mean(d_scaled * scaled, axis=-1, keepdims=True)
    )
    return (d_inputs, d_gain, d_offset)


def masked_scores(queries, key_rows, segment):
    raw_scores = jnp.einsum("qhd,khd->hqk", queries, key_rows, preferred_element_type=jnp.float32)
    same_doc = segment[:, None] == segment[None, :]
    return jnp.where(same_doc[None], raw_scores * HEAD_DIM ** (-0.5), -1000000000.0)


def attend_forward(block):
    queries, key_rows, value_rows, segment = block
    scores = masked_scores(queries, key_rows, segment)
    row_max = jnp.max(scores, axis=-1, keepdims=True)
    exponent = jnp.exp(scores - row_max)
    row_total = jnp.sum(exponent, axis=-1, keepdims=True)
    probabilities = (exponent / row_total).astype(jnp.bfloat16)
    context = jnp.einsum(
        "hqk,khd->qhd", probabilities, value_rows, preferred_element_type=jnp.float32
    )
    return (context.astype(jnp.bfloat16), row_max[..., 0] + jnp.log(row_total[..., 0]))


def attend_backward(block):
    queries, key_rows, value_rows, segment, logsum, d_context = block
    scores = masked_scores(queries, key_rows, segment)
    probabilities = jnp.exp(scores - logsum[..., None])
    d_probs = jnp.einsum("qhd,khd->hqk", d_context, value_rows, preferred_element_type=jnp.float32)
    row_dot = jnp.sum(d_probs * probabilities, axis=-1, keepdims=True)
    d_raw = (probabilities * (d_probs - row_dot) * HEAD_DIM ** (-0.5)).astype(jnp.bfloat16)
    d_queries = jnp.einsum("hqk,khd->qhd", d_raw, key_rows, preferred_element_type=jnp.float32)
    d_keys = jnp.einsum("hqk,qhd->khd", d_raw, queries, preferred_element_type=jnp.float32)
    d_values = jnp.einsum(
        "hqk,qhd->khd",
        probabilities.astype(jnp.bfloat16),
        d_context,
        preferred_element_type=jnp.float32,
    )
    return (
        d_queries.astype(jnp.bfloat16),
        d_keys.astype(jnp.bfloat16),
        d_values.astype(jnp.bfloat16),
    )


def tensor_plan(
    tokens,
    segments,
    w_qkv,
    bias_qv,
    w_out,
    bias_out,
    ln1_gain,
    ln1_bias,
    w_up,
    bias_up,
    w_down,
    bias_down,
    ln2_gain,
    ln2_bias,
    d_out,
):
    qkv_w, out_w, up_w, down_w = (
        lax.all_gather(w_qkv, "dp", axis=1, tiled=True),
        lax.all_gather(w_out, "dp", axis=1, tiled=True),
        lax.all_gather(w_up, "dp", axis=0, tiled=True),
        lax.all_gather(w_down, "dp", axis=1, tiled=True),
    )
    head_width = qkv_w.shape[2]
    unit_width = up_w.shape[1]
    tensor_index = lax.axis_index("tensor")
    bias_query = lax.dynamic_slice_in_dim(bias_qv[0], tensor_index * head_width, head_width)
    bias_value = lax.dynamic_slice_in_dim(bias_qv[1], tensor_index * head_width, head_width)
    bias_units = lax.dynamic_slice_in_dim(bias_up, tensor_index * unit_width, unit_width)
    block_rows = lax.all_gather(tokens, "tensor", axis=0, tiled=True)
    pieces = [
        matmul(block_rows, qkv_w[0]) + bias_query,
        matmul(block_rows, qkv_w[1]),
        matmul(block_rows, qkv_w[2]) + bias_value,
    ]
    qkv_all = jnp.concatenate(pieces, axis=1)
    qkv_rows = qkv_all.astype(jnp.bfloat16)
    group_rows = qkv_rows.shape[0]
    shape_seq = (segments.shape[0], SEQ, head_width // HEAD_DIM, HEAD_DIM)
    queries = qkv_rows[:, :head_width].reshape(shape_seq)
    key_rows = qkv_rows[:, head_width : 2 * head_width].reshape(shape_seq)
    value_rows = qkv_rows[:, 2 * head_width :].reshape(shape_seq)
    context, logsum = lax.map(attend_forward, (queries, key_rows, value_rows, segments))
    context_rows = context.reshape(group_rows, head_width)
    attn_rows = lax.psum_scatter(
        matmul(context_rows, out_w).astype(jnp.bfloat16), "tensor", scatter_dimension=0, tiled=True
    ).astype(jnp.float32)
    z_one = tokens.astype(jnp.float32) + attn_rows + bias_out
    h_one, scaled_one, spread_one = norm_forward(z_one, ln1_gain, ln1_bias)
    h_low = h_one.astype(jnp.bfloat16)
    pieces = [matmul(lax.all_gather(h_low, "tensor", axis=0, tiled=True), up_w) + bias_units]
    up_all = pieces[0]
    activation = jax.nn.gelu(up_all, approximate=False).astype(jnp.bfloat16)
    mlp_rows = lax.psum_scatter(
        matmul(activation, down_w).astype(jnp.bfloat16), "tensor", scatter_dimension=0, tiled=True
    ).astype(jnp.float32)
    z_two = h_one + mlp_rows + bias_down
    normed, scaled_two, spread_two = norm_forward(z_two, ln2_gain, ln2_bias)
    output = normed.astype(jnp.bfloat16)
    qkv_w, out_w, up_w, down_w = (
        lax.all_gather(w_qkv, "dp", axis=1, tiled=True),
        lax.all_gather(w_out, "dp", axis=1, tiled=True),
        lax.all_gather(w_up, "dp", axis=0, tiled=True),
        lax.all_gather(w_down, "dp", axis=1, tiled=True),
    )
    grad_two, d_gain_two, d_offset_two = norm_backward(
        d_out.astype(jnp.float32), scaled_two, spread_two, ln2_gain
    )
    d_bias_down = jnp.sum(grad_two, axis=0)
    grad_two_low = grad_two.astype(jnp.bfloat16)
    block_rows = lax.all_gather(grad_two_low, "tensor", axis=0, tiled=True)
    d_act = outer_cols(block_rows, down_w)
    d_wdown, d_act = (inner_rows(activation, block_rows), d_act)
    gelu_pull = jax.vjp(lambda inputs: jax.nn.gelu(inputs, approximate=False), up_all)[1]
    d_up = gelu_pull(d_act)[0].astype(jnp.bfloat16)
    d_bias_units = jnp.sum(d_up, axis=0, dtype=jnp.float32)
    d_bias_up = lax.dynamic_update_slice_in_dim(
        jnp.zeros(bias_up.shape, jnp.float32), d_bias_units, tensor_index * unit_width, 0
    )
    mlp_back = lax.psum_scatter(
        outer_cols(d_up, up_w).astype(jnp.bfloat16), "tensor", scatter_dimension=0, tiled=True
    ).astype(jnp.float32)
    d_wup = inner_rows(lax.all_gather(h_low, "tensor", axis=0, tiled=True), d_up)
    grad_one, d_gain_one, d_offset_one = norm_backward(
        mlp_back + grad_two, scaled_one, spread_one, ln1_gain
    )
    d_bias_out = jnp.sum(grad_one, axis=0)
    grad_one_low = grad_one.astype(jnp.bfloat16)
    block_rows = lax.all_gather(grad_one_low, "tensor", axis=0, tiled=True)
    d_ctx = outer_cols(block_rows, out_w)
    d_wout, d_ctx = (inner_rows(context_rows, block_rows), d_ctx)
    d_ctx_low = d_ctx.astype(jnp.bfloat16).reshape(shape_seq)
    d_queries, d_keys, d_values = lax.map(
        attend_backward, (queries, key_rows, value_rows, segments, logsum, d_ctx_low)
    )
    d_qkv = jnp.concatenate(
        [
            d_queries.reshape(group_rows, head_width),
            d_keys.reshape(group_rows, head_width),
            d_values.reshape(group_rows, head_width),
        ],
        axis=1,
    )
    bias_pair = jnp.stack(
        [
            jnp.sum(d_qkv[:, :head_width], axis=0, dtype=jnp.float32),
            jnp.sum(d_qkv[:, 2 * head_width :], axis=0, dtype=jnp.float32),
        ]
    )
    d_bias_qv = lax.dynamic_update_slice_in_dim(
        jnp.zeros(bias_qv.shape, jnp.float32), bias_pair, tensor_index * head_width, 1
    )
    total_rows = outer_cols(d_qkv[:, :head_width], qkv_w[0])
    total_rows = total_rows + outer_cols(d_qkv[:, head_width : 2 * head_width], qkv_w[1])
    attn_back = lax.psum_scatter(
        (total_rows + outer_cols(d_qkv[:, 2 * head_width :], qkv_w[2])).astype(jnp.bfloat16),
        "tensor",
        scatter_dimension=0,
        tiled=True,
    ).astype(jnp.float32)
    grad_tokens = attn_back + grad_one
    block_rows = lax.all_gather(tokens, "tensor", axis=0, tiled=True)
    grads_part = d_qkv
    grads_part = grads_part.reshape(block_rows.shape[0], 3, head_width)
    d_wqkv = jnp.einsum("rd,rtc->tdc", block_rows, grads_part, preferred_element_type=jnp.float32)
    grad_w_qkv, grad_w_out, grad_w_up, grad_w_down = (
        lax.psum_scatter(d_wqkv.astype(jnp.bfloat16), "dp", scatter_dimension=1, tiled=True).astype(
            jnp.float32
        ),
        lax.psum_scatter(d_wout.astype(jnp.bfloat16), "dp", scatter_dimension=1, tiled=True).astype(
            jnp.float32
        ),
        lax.psum_scatter(d_wup.astype(jnp.bfloat16), "dp", scatter_dimension=0, tiled=True).astype(
            jnp.float32
        ),
        lax.psum_scatter(
            d_wdown.astype(jnp.bfloat16), "dp", scatter_dimension=1, tiled=True
        ).astype(jnp.float32),
    )
    small_grads = lax.psum(
        (
            d_bias_qv,
            d_bias_out,
            d_gain_one,
            d_offset_one,
            d_bias_up,
            d_bias_down,
            d_gain_two,
            d_offset_two,
        ),
        ("dp", "tensor"),
    )
    return (
        output,
        grad_tokens,
        grad_w_qkv,
        small_grads[0],
        grad_w_out,
        small_grads[1],
        small_grads[2],
        small_grads[3],
        grad_w_up,
        small_grads[4],
        grad_w_down,
        small_grads[5],
        small_grads[6],
        small_grads[7],
    )


def swap(array, name, mask):
    size = lax.axis_size(name)
    return lax.ppermute(array, name, [(index, index ^ mask) for index in range(size)])


def over_y(array):
    return swap(array, "tensor", 1)


def over_x(array):
    return swap(array, "dp", 2)


def over_core(array):
    return swap(array, "dp", 1)


def over_z(array, step):
    return swap(array, "dp", 4 * step)


def gather_weight(shard):
    half_rows = shard.shape[0] // 2
    stack = [shard] + [over_z(shard, step) for step in (1, 2, 3)]
    halves = []
    for half, first, second in ((0, over_x, over_y), (1, over_y, over_x)):
        own = jnp.concatenate([part[half * half_rows :][:half_rows] for part in stack], axis=0)
        near = first(own)
        side = second(own)
        both = second(near)
        parts = [own, near, side, both] if half == 0 else [own, side, near, both]
        halves.append((parts, [over_core(part) for part in parts]))
    return [
        jnp.concatenate(
            [
                part
                for here, there in halves
                for part in here[2 * group : 2 * group + 2] + there[2 * group : 2 * group + 2]
            ],
            axis=0,
        )
        for group in (0, 1)
    ]


def add_low(left, right):
    return (left.astype(jnp.float32) + right.astype(jnp.float32)).astype(jnp.bfloat16)


def scatter_grad(groups):
    rows, columns = groups[0].shape
    sums = []
    for half in (0, 1):
        blocks = [group.reshape(2, 2, 2, rows // 8, columns)[half] for group in groups]
        others = [over_core(block[1]) for block in blocks]
        blocks = [add_low(block[0], other) for block, other in zip(blocks, others)]
        if half == 0:
            block = add_low(blocks[0], over_y(blocks[1]))
            block = add_low(block[0], over_x(block[1]))
        else:
            others = [over_x(block[1]) for block in blocks]
            blocks = [add_low(block[0], other) for block, other in zip(blocks, others)]
            block = add_low(blocks[0], over_y(blocks[1]))
        sums.append(block.reshape(4, rows // 32, columns))
    stack = jnp.concatenate(sums, axis=1)
    parts = [stack[0]] + [over_z(stack[step], step) for step in (1, 2, 3)]
    parts = [part.astype(jnp.float32) for part in parts]
    return (parts[0] + parts[1]) + (parts[2] + parts[3])


def sum_all(array):
    array = (array + over_z(array, 1)) + (over_z(array, 2) + over_z(array, 3))
    beside = over_y(array)
    array = (array + over_x(array)) + (beside + over_x(beside))
    return array + over_core(array)


def head_scores(queries, key_rows, same_doc):
    raw_scores = outer_cols(queries * jnp.bfloat16(HEAD_DIM ** (-0.5)), key_rows)
    return jnp.where(same_doc, raw_scores, -1000000000.0)


def attend_forward_kernel(q_ref, k_ref, v_ref, column_ref, row_ref, ctx_ref, logsum_ref):
    lane = lax.broadcasted_iota(jnp.int32, q_ref.shape, 1) // HEAD_DIM
    same_doc = column_ref[...] == row_ref[...]
    value_rows = v_ref[...]
    contexts = []
    logsums = []
    for head in (0, 1):
        queries = jnp.where(lane == head, q_ref[...], jnp.bfloat16(0))
        scores = head_scores(queries, k_ref[...], same_doc)
        row_max = jnp.max(scores, axis=-1, keepdims=True)
        exponent = jnp.exp(scores - row_max)
        row_total = jnp.sum(exponent, axis=-1, keepdims=True)
        probabilities = (exponent * (1.0 / row_total)).astype(jnp.bfloat16)
        contexts.append(matmul(probabilities, value_rows))
        logsums.append(row_max + jnp.log(row_total))
    ctx_ref[...] = jnp.where(lane == 0, contexts[0], contexts[1]).astype(jnp.bfloat16)
    logsum_ref[...] = jnp.where(lane == 0, logsums[0], logsums[1])


def attend_backward_kernel(
    q_ref, k_ref, v_ref, column_ref, row_ref, logsum_ref, dctx_ref, dq_ref, dk_ref, dv_ref
):
    lane = lax.broadcasted_iota(jnp.int32, q_ref.shape, 1) // HEAD_DIM
    same_doc = column_ref[...] == row_ref[...]
    key_rows = k_ref[...]
    value_rows = v_ref[...]
    results = []
    for head in (0, 1):
        queries = jnp.where(lane == head, q_ref[...], jnp.bfloat16(0))
        d_context = jnp.where(lane == head, dctx_ref[...], jnp.bfloat16(0))
        scores = head_scores(queries, key_rows, same_doc)
        place = head * HEAD_DIM
        probabilities = jnp.exp(scores - logsum_ref[:, place : place + 1])
        d_probs = outer_cols(d_context, value_rows)
        row_dot = jnp.sum(d_probs * probabilities, axis=-1, keepdims=True)
        d_raw = (probabilities * (d_probs - row_dot) * HEAD_DIM ** (-0.5)).astype(jnp.bfloat16)
        results.append(
            (
                matmul(d_raw, key_rows),
                inner_rows(d_raw, queries),
                inner_rows(probabilities.astype(jnp.bfloat16), d_context),
            )
        )
    for ref, left, right in zip((dq_ref, dk_ref, dv_ref), *results):
        ref[...] = jnp.where(lane == 0, left, right).astype(jnp.bfloat16)


def attention_specs(rows, width, start):
    return pl.BlockSpec((rows, width), lambda pair, start=start: (0, start + pair))


def attend_rows_forward(qkv, column, row):
    rows, pairs = qkv.shape[0], qkv.shape[1] // 384
    whole = [pl.BlockSpec(column.shape, lambda pair: (0, 0)), pl.BlockSpec(row.shape, lambda pair: (0, 0))]
    return pl.pallas_call(
        attend_forward_kernel,
        grid=(pairs,),
        in_specs=[attention_specs(rows, 128, part * pairs) for part in range(3)] + whole,
        out_specs=[attention_specs(rows, 128, 0)] * 2,
        out_shape=[
            jax.ShapeDtypeStruct((rows, pairs * 128), jnp.bfloat16),
            jax.ShapeDtypeStruct((rows, pairs * 128), jnp.float32),
        ],
        cost_estimate=pl.CostEstimate(
            flops=8 * pairs * rows * rows * 128,
            bytes_accessed=pairs * rows * 128 * 12,
            transcendentals=2 * pairs * rows * rows,
        ),
        compiler_params=pltpu.CompilerParams(vmem_limit_bytes=24 << 20),
    )(qkv, qkv, qkv, column, row)


def attend_rows_backward(qkv, column, row, logsum, d_context):
    rows, pairs = qkv.shape[0], qkv.shape[1] // 384
    whole = [pl.BlockSpec(column.shape, lambda pair: (0, 0)), pl.BlockSpec(row.shape, lambda pair: (0, 0))]
    return pl.pallas_call(
        attend_backward_kernel,
        grid=(pairs,),
        in_specs=[attention_specs(rows, 128, part * pairs) for part in range(3)]
        + whole
        + [attention_specs(rows, 128, 0)] * 2,
        out_specs=[attention_specs(rows, 128, 0)] * 3,
        out_shape=[jax.ShapeDtypeStruct((rows, pairs * 128), jnp.bfloat16)] * 3,
        cost_estimate=pl.CostEstimate(
            flops=20 * pairs * rows * rows * 128,
            bytes_accessed=pairs * rows * 128 * 18,
            transcendentals=2 * pairs * rows * rows,
        ),
        compiler_params=pltpu.CompilerParams(vmem_limit_bytes=32 << 20),
    )(qkv, qkv, qkv, column, row, logsum, d_context)


def gelu_pair(inputs):
    share = 0.5 * (1.0 + lax.erf(inputs * 0.5**0.5))
    slope = share + inputs * (jnp.exp(-0.5 * inputs * inputs) * (0.5 / jnp.pi) ** 0.5)
    return (inputs * share).astype(jnp.bfloat16), slope.astype(jnp.bfloat16)


def data_plan(
    tokens,
    segments,
    w_qkv,
    bias_qv,
    w_out,
    bias_out,
    ln1_gain,
    ln1_bias,
    w_up,
    bias_up,
    w_down,
    bias_down,
    ln2_gain,
    ln2_bias,
    d_out,
):
    low, wide = jnp.bfloat16, jnp.float32
    dp_index = lax.axis_index("dp")
    tensor_index = lax.axis_index("tensor")
    width = tokens.shape[1]
    head_width = w_qkv.shape[2]
    unit_width = w_up.shape[1]
    groups = (0, 1)

    qkv_w = gather_weight(jnp.concatenate([w_qkv[0], w_qkv[1], w_qkv[2]], axis=1))
    out_w = gather_weight(w_out.T)
    up_w = gather_weight(w_up)
    down_w = gather_weight(w_down.T)

    place = jnp.arange(width)
    block = ((place // 32) % 4) * 4 + ((place // 128) % 2) * 2 + (place // 256) % 2
    source = (dp_index ^ block) * 64 + (place // 512) * 32 + place % 32
    order = (jnp.arange(width)[:, None] == source[None, :]).astype(low)

    def group_of(vector, group, size):
        return lax.dynamic_slice_in_dim(vector, (tensor_index ^ group) * size, size, axis=-1)

    def whole_of(parts):
        left, right = parts
        return jnp.where(
            tensor_index == 0,
            jnp.concatenate([left, right], axis=-1),
            jnp.concatenate([right, left], axis=-1),
        )

    vectors = jnp.dot(
        jnp.stack([bias_out, ln1_gain, ln1_bias, bias_down, ln2_gain, ln2_bias]),
        order.astype(wide),
        precision=lax.Precision.HIGHEST,
    )
    bias_out, ln1_gain, ln1_bias, bias_down, ln2_gain, ln2_bias = [vectors[i] for i in range(6)]
    own_rows = matmul(tokens, order).astype(low)
    cotangent = matmul(d_out, order)

    which = lax.dynamic_slice_in_dim(segments, tensor_index, 1, axis=0)
    column, row = which.reshape(SEQ, 1), which

    qkv, context, logsum = [], [], []
    for group in groups:
        bias = jnp.concatenate(
            [
                group_of(bias_qv[0], group, head_width),
                jnp.zeros((head_width,), wide),
                group_of(bias_qv[1], group, head_width),
            ]
        )
        qkv.append((matmul(own_rows, qkv_w[group]) + bias).astype(low))
        ctx, total = attend_rows_forward(qkv[group], column, row)
        context.append(ctx)
        logsum.append(total)
    attn_rows = outer_cols(context[0], out_w[0]) + outer_cols(context[1], out_w[1])
    z_one = own_rows.astype(wide) + attn_rows + bias_out
    h_one, scaled_one, spread_one = norm_forward(z_one, ln1_gain, ln1_bias)
    h_low = h_one.astype(low)
    activation, slope = [], []
    for group in groups:
        units = matmul(h_low, up_w[group]) + group_of(bias_up, group, unit_width)
        pair = gelu_pair(units)
        activation.append(pair[0])
        slope.append(pair[1])
    mlp_rows = outer_cols(activation[0], down_w[0]) + outer_cols(activation[1], down_w[1])
    z_two = h_one + mlp_rows + bias_down
    normed, scaled_two, spread_two = norm_forward(z_two, ln2_gain, ln2_bias)
    output = outer_cols(normed.astype(low), order).astype(low)

    grad_two, d_gain_two, d_offset_two = norm_backward(cotangent, scaled_two, spread_two, ln2_gain)
    d_bias_down = jnp.sum(grad_two, axis=0)
    grad_two_low = grad_two.astype(low)
    grad_w_down = scatter_grad([inner_rows(grad_two_low, activation[g]).astype(low) for g in groups]).T
    d_up = [(matmul(grad_two_low, down_w[g]) * slope[g].astype(wide)).astype(low) for g in groups]
    d_bias_up = whole_of([jnp.sum(d_up[g], axis=0, dtype=wide) for g in groups])
    grad_w_up = scatter_grad([inner_rows(h_low, d_up[g]).astype(low) for g in groups])
    mlp_back = outer_cols(d_up[0], up_w[0]) + outer_cols(d_up[1], up_w[1])
    grad_one, d_gain_one, d_offset_one = norm_backward(
        mlp_back + grad_two, scaled_one, spread_one, ln1_gain
    )
    d_bias_out = jnp.sum(grad_one, axis=0)
    grad_one_low = grad_one.astype(low)
    grad_w_out = scatter_grad([inner_rows(grad_one_low, context[g]).astype(low) for g in groups]).T
    d_qkv = []
    for group in groups:
        d_ctx = matmul(grad_one_low, out_w[group]).astype(low)
        d_qkv.append(
            jnp.concatenate(
                attend_rows_backward(qkv[group], column, row, logsum[group], d_ctx), axis=1
            )
        )
    grad_qkv = scatter_grad([inner_rows(own_rows, d_qkv[g]).astype(low) for g in groups])
    grad_w_qkv = jnp.stack([grad_qkv[:, i * head_width : (i + 1) * head_width] for i in range(3)])
    attn_back = outer_cols(d_qkv[0], qkv_w[0]) + outer_cols(d_qkv[1], qkv_w[1])
    grad_rows = attn_back + grad_one
    upper = grad_rows.astype(low)
    lower = (grad_rows - upper.astype(wide)).astype(low)
    grad_tokens = outer_cols(upper, order) + outer_cols(lower, order)

    sums = [jnp.sum(d_qkv[g], axis=0, dtype=wide) for g in groups]
    d_bias_q = whole_of([s[:head_width] for s in sums])
    d_bias_v = whole_of([s[2 * head_width :] for s in sums])
    narrow = jnp.dot(
        jnp.stack([d_bias_out, d_gain_one, d_offset_one, d_bias_down, d_gain_two, d_offset_two]),
        order.astype(wide).T,
        precision=lax.Precision.HIGHEST,
    )
    small = sum_all(
        jnp.concatenate([narrow, d_bias_q[None], d_bias_v[None], d_bias_up.reshape(-1, width)], axis=0)
    )
    return (
        output,
        grad_tokens,
        grad_w_qkv,
        small[6:8],
        grad_w_out,
        small[0],
        small[1],
        small[2],
        grad_w_up,
        small[8:].reshape(-1),
        grad_w_down,
        small[3],
        small[4],
        small[5],
    )


def local(*arrays):
    tokens = arrays[0]
    sizes = (lax.axis_size("dp"), lax.axis_size("tensor"))
    if sizes == (16, 2) and tokens.shape == (SEQ, 1024):
        return data_plan(*arrays)
    return tensor_plan(*arrays)


def solution(mesh):
    return jax.shard_map(
        local,
        mesh=mesh,
        in_specs=(
            P(("dp", "tensor"), None),
            P("dp", None),
            P(None, "dp", "tensor"),
            P(),
            P("tensor", "dp"),
            P(),
            P(),
            P(),
            P("dp", "tensor"),
            P(),
            P("tensor", "dp"),
            P(),
            P(),
            P(),
            P(("dp", "tensor"), None),
        ),
        out_specs=(
            P(("dp", "tensor"), None),
            P(("dp", "tensor"), None),
            P(None, "dp", "tensor"),
            P(),
            P("tensor", "dp"),
            P(),
            P(),
            P(),
            P("dp", "tensor"),
            P(),
            P("tensor", "dp"),
            P(),
            P(),
            P(),
        ),
        check_vma=False,
    )
```

```python
import functools

import jax
import jax.numpy as jnp
from jax import lax
from jax.experimental import pallas as pl
from jax.experimental.pallas import tpu as pltpu
from jax.sharding import PartitionSpec as P

HEAD_DIM = 64
SEQ = 512


eps = 1e-12


def matmul(left, right):
    return jnp.dot(left, right, preferred_element_type=jnp.float32)


def inner_rows(left, right):
    return lax.dot_general(
        left, right, (((0,), (0,)), ((), ())), preferred_element_type=jnp.float32
    )


def outer_cols(left, right):
    return lax.dot_general(
        left, right, (((1,), (1,)), ((), ())), preferred_element_type=jnp.float32
    )


def norm_forward(inputs, gain_vec, offset):
    center = jnp.mean(inputs, axis=-1, keepdims=True)
    spread = lax.rsqrt(jnp.mean(jnp.square(inputs - center), axis=-1, keepdims=True) + eps)
    scaled = (inputs - center) * spread
    return (scaled * gain_vec + offset, scaled, spread)


def norm_backward(gradient, scaled, spread, gain_vec):
    d_gain = jnp.sum(gradient * scaled, axis=0)
    d_offset = jnp.sum(gradient, axis=0)
    d_scaled = gradient * gain_vec
    d_inputs = spread * (
        d_scaled
        - jnp.mean(d_scaled, axis=-1, keepdims=True)
        - scaled * jnp.mean(d_scaled * scaled, axis=-1, keepdims=True)
    )
    return (d_inputs, d_gain, d_offset)


def masked_scores(queries, key_rows, segment):
    raw_scores = jnp.einsum("qhd,khd->hqk", queries, key_rows, preferred_element_type=jnp.float32)
    same_doc = segment[:, None] == segment[None, :]
    return jnp.where(same_doc[None], raw_scores * HEAD_DIM ** (-0.5), -1000000000.0)


def attend_forward(block):
    queries, key_rows, value_rows, segment = block
    scores = masked_scores(queries, key_rows, segment)
    row_max = jnp.max(scores, axis=-1, keepdims=True)
    exponent = jnp.exp(scores - row_max)
    row_total = jnp.sum(exponent, axis=-1, keepdims=True)
    probabilities = (exponent / row_total).astype(jnp.bfloat16)
    context = jnp.einsum(
        "hqk,khd->qhd", probabilities, value_rows, preferred_element_type=jnp.float32
    )
    return (context.astype(jnp.bfloat16), row_max[..., 0] + jnp.log(row_total[..., 0]))


def attend_backward(block):
    queries, key_rows, value_rows, segment, logsum, d_context = block
    scores = masked_scores(queries, key_rows, segment)
    probabilities = jnp.exp(scores - logsum[..., None])
    d_probs = jnp.einsum("qhd,khd->hqk", d_context, value_rows, preferred_element_type=jnp.float32)
    row_dot = jnp.sum(d_probs * probabilities, axis=-1, keepdims=True)
    d_raw = (probabilities * (d_probs - row_dot) * HEAD_DIM ** (-0.5)).astype(jnp.bfloat16)
    d_queries = jnp.einsum("hqk,khd->qhd", d_raw, key_rows, preferred_element_type=jnp.float32)
    d_keys = jnp.einsum("hqk,qhd->khd", d_raw, queries, preferred_element_type=jnp.float32)
    d_values = jnp.einsum(
        "hqk,qhd->khd",
        probabilities.astype(jnp.bfloat16),
        d_context,
        preferred_element_type=jnp.float32,
    )
    return (
        d_queries.astype(jnp.bfloat16),
        d_keys.astype(jnp.bfloat16),
        d_values.astype(jnp.bfloat16),
    )


def tensor_plan(
    tokens,
    segments,
    w_qkv,
    bias_qv,
    w_out,
    bias_out,
    ln1_gain,
    ln1_bias,
    w_up,
    bias_up,
    w_down,
    bias_down,
    ln2_gain,
    ln2_bias,
    d_out,
):
    qkv_w, out_w, up_w, down_w = (
        lax.all_gather(w_qkv, "dp", axis=1, tiled=True),
        lax.all_gather(w_out, "dp", axis=1, tiled=True),
        lax.all_gather(w_up, "dp", axis=0, tiled=True),
        lax.all_gather(w_down, "dp", axis=1, tiled=True),
    )
    head_width = qkv_w.shape[2]
    unit_width = up_w.shape[1]
    tensor_index = lax.axis_index("tensor")
    bias_query = lax.dynamic_slice_in_dim(bias_qv[0], tensor_index * head_width, head_width)
    bias_value = lax.dynamic_slice_in_dim(bias_qv[1], tensor_index * head_width, head_width)
    bias_units = lax.dynamic_slice_in_dim(bias_up, tensor_index * unit_width, unit_width)
    block_rows = lax.all_gather(tokens, "tensor", axis=0, tiled=True)
    pieces = [
        matmul(block_rows, qkv_w[0]) + bias_query,
        matmul(block_rows, qkv_w[1]),
        matmul(block_rows, qkv_w[2]) + bias_value,
    ]
    qkv_all = jnp.concatenate(pieces, axis=1)
    qkv_rows = qkv_all.astype(jnp.bfloat16)
    group_rows = qkv_rows.shape[0]
    shape_seq = (segments.shape[0], SEQ, head_width // HEAD_DIM, HEAD_DIM)
    queries = qkv_rows[:, :head_width].reshape(shape_seq)
    key_rows = qkv_rows[:, head_width : 2 * head_width].reshape(shape_seq)
    value_rows = qkv_rows[:, 2 * head_width :].reshape(shape_seq)
    context, logsum = lax.map(attend_forward, (queries, key_rows, value_rows, segments))
    context_rows = context.reshape(group_rows, head_width)
    attn_rows = lax.psum_scatter(
        matmul(context_rows, out_w).astype(jnp.bfloat16), "tensor", scatter_dimension=0, tiled=True
    ).astype(jnp.float32)
    z_one = tokens.astype(jnp.float32) + attn_rows + bias_out
    h_one, scaled_one, spread_one = norm_forward(z_one, ln1_gain, ln1_bias)
    h_low = h_one.astype(jnp.bfloat16)
    pieces = [matmul(lax.all_gather(h_low, "tensor", axis=0, tiled=True), up_w) + bias_units]
    up_all = pieces[0]
    activation = jax.nn.gelu(up_all, approximate=False).astype(jnp.bfloat16)
    mlp_rows = lax.psum_scatter(
        matmul(activation, down_w).astype(jnp.bfloat16), "tensor", scatter_dimension=0, tiled=True
    ).astype(jnp.float32)
    z_two = h_one + mlp_rows + bias_down
    normed, scaled_two, spread_two = norm_forward(z_two, ln2_gain, ln2_bias)
    output = normed.astype(jnp.bfloat16)
    qkv_w, out_w, up_w, down_w = (
        lax.all_gather(w_qkv, "dp", axis=1, tiled=True),
        lax.all_gather(w_out, "dp", axis=1, tiled=True),
        lax.all_gather(w_up, "dp", axis=0, tiled=True),
        lax.all_gather(w_down, "dp", axis=1, tiled=True),
    )
    grad_two, d_gain_two, d_offset_two = norm_backward(
        d_out.astype(jnp.float32), scaled_two, spread_two, ln2_gain
    )
    d_bias_down = jnp.sum(grad_two, axis=0)
    grad_two_low = grad_two.astype(jnp.bfloat16)
    block_rows = lax.all_gather(grad_two_low, "tensor", axis=0, tiled=True)
    d_act = outer_cols(block_rows, down_w)
    d_wdown, d_act = (inner_rows(activation, block_rows), d_act)
    gelu_pull = jax.vjp(lambda inputs: jax.nn.gelu(inputs, approximate=False), up_all)[1]
    d_up = gelu_pull(d_act)[0].astype(jnp.bfloat16)
    d_bias_units = jnp.sum(d_up, axis=0, dtype=jnp.float32)
    d_bias_up = lax.dynamic_update_slice_in_dim(
        jnp.zeros(bias_up.shape, jnp.float32), d_bias_units, tensor_index * unit_width, 0
    )
    mlp_back = lax.psum_scatter(
        outer_cols(d_up, up_w).astype(jnp.bfloat16), "tensor", scatter_dimension=0, tiled=True
    ).astype(jnp.float32)
    d_wup = inner_rows(lax.all_gather(h_low, "tensor", axis=0, tiled=True), d_up)
    grad_one, d_gain_one, d_offset_one = norm_backward(
        mlp_back + grad_two, scaled_one, spread_one, ln1_gain
    )
    d_bias_out = jnp.sum(grad_one, axis=0)
    grad_one_low = grad_one.astype(jnp.bfloat16)
    block_rows = lax.all_gather(grad_one_low, "tensor", axis=0, tiled=True)
    d_ctx = outer_cols(block_rows, out_w)
    d_wout, d_ctx = (inner_rows(context_rows, block_rows), d_ctx)
    d_ctx_low = d_ctx.astype(jnp.bfloat16).reshape(shape_seq)
    d_queries, d_keys, d_values = lax.map(
        attend_backward, (queries, key_rows, value_rows, segments, logsum, d_ctx_low)
    )
    d_qkv = jnp.concatenate(
        [
            d_queries.reshape(group_rows, head_width),
            d_keys.reshape(group_rows, head_width),
            d_values.reshape(group_rows, head_width),
        ],
        axis=1,
    )
    bias_pair = jnp.stack(
        [
            jnp.sum(d_qkv[:, :head_width], axis=0, dtype=jnp.float32),
            jnp.sum(d_qkv[:, 2 * head_width :], axis=0, dtype=jnp.float32),
        ]
    )
    d_bias_qv = lax.dynamic_update_slice_in_dim(
        jnp.zeros(bias_qv.shape, jnp.float32), bias_pair, tensor_index * head_width, 1
    )
    total_rows = outer_cols(d_qkv[:, :head_width], qkv_w[0])
    total_rows = total_rows + outer_cols(d_qkv[:, head_width : 2 * head_width], qkv_w[1])
    attn_back = lax.psum_scatter(
        (total_rows + outer_cols(d_qkv[:, 2 * head_width :], qkv_w[2])).astype(jnp.bfloat16),
        "tensor",
        scatter_dimension=0,
        tiled=True,
    ).astype(jnp.float32)
    grad_tokens = attn_back + grad_one
    block_rows = lax.all_gather(tokens, "tensor", axis=0, tiled=True)
    grads_part = d_qkv
    grads_part = grads_part.reshape(block_rows.shape[0], 3, head_width)
    d_wqkv = jnp.einsum("rd,rtc->tdc", block_rows, grads_part, preferred_element_type=jnp.float32)
    grad_w_qkv, grad_w_out, grad_w_up, grad_w_down = (
        lax.psum_scatter(d_wqkv.astype(jnp.bfloat16), "dp", scatter_dimension=1, tiled=True).astype(
            jnp.float32
        ),
        lax.psum_scatter(d_wout.astype(jnp.bfloat16), "dp", scatter_dimension=1, tiled=True).astype(
            jnp.float32
        ),
        lax.psum_scatter(d_wup.astype(jnp.bfloat16), "dp", scatter_dimension=0, tiled=True).astype(
            jnp.float32
        ),
        lax.psum_scatter(
            d_wdown.astype(jnp.bfloat16), "dp", scatter_dimension=1, tiled=True
        ).astype(jnp.float32),
    )
    small_grads = lax.psum(
        (
            d_bias_qv,
            d_bias_out,
            d_gain_one,
            d_offset_one,
            d_bias_up,
            d_bias_down,
            d_gain_two,
            d_offset_two,
        ),
        ("dp", "tensor"),
    )
    return (
        output,
        grad_tokens,
        grad_w_qkv,
        small_grads[0],
        grad_w_out,
        small_grads[1],
        small_grads[2],
        small_grads[3],
        grad_w_up,
        small_grads[4],
        grad_w_down,
        small_grads[5],
        small_grads[6],
        small_grads[7],
    )


def swap(array, name, mask):
    size = lax.axis_size(name)
    return lax.ppermute(array, name, [(index, index ^ mask) for index in range(size)])


def over_y(array):
    return swap(array, "tensor", 1)


def over_x(array):
    return swap(array, "dp", 2)


def over_core(array):
    return swap(array, "dp", 1)


def over_z(array, step):
    return swap(array, "dp", 4 * step)


def gather_first(stack):
    rows = stack[0].shape[0] // 2
    left, right = [jnp.concatenate([part[half * rows :][:rows] for part in stack]) for half in (0, 1)]
    return left, over_x(left), right, over_y(right)


def gather_second(parts):
    left = jnp.concatenate(parts[:2])
    right = jnp.concatenate(parts[2:])
    return left, over_y(left), right, over_x(right), over_core(left), over_core(right)


def gather_last(parts):
    left, left_other, right, right_other, left_core, right_core = parts
    here = (left, left_other, right, right_other)
    return here + (left_core, over_core(left_other), right_core, over_core(right_other))


def gather_weights(shards, first_work, second_work):
    after = lax.optimization_barrier
    one, two, three = shards
    one = [one] + [over_z(one, step) for step in (1, 2, 3)]
    two = [two, over_z(two, 1)]
    one, two, three = after((one, two, three))
    one = gather_first(one)
    two = two + [over_z(two[0], 2)]
    three = [three, over_z(three, 1)]
    one, two, three = after((one, two, three))
    one = gather_second(one)
    two = two + [over_z(two[1], 2)]
    one, two, three = after((one, two, three))
    two = gather_first(two)
    one = gather_last(one)
    three = three + [over_z(three[0], 2)]
    one, two, three = after((one, two, three))
    two = gather_second(two)
    three = three + [over_z(three[1], 2)]
    made = first_work(one)
    two, three, made = after((two, three, made))
    three = gather_first(three)
    two = gather_last(two)
    two, three, made = after((two, three, made))
    three = gather_second(three)
    made = second_work(two, made)
    three, made = after((three, made))
    return (one, two, gather_last(three)), made


def add_low(left, right):
    return (left.astype(jnp.float32) + right.astype(jnp.float32)).astype(jnp.bfloat16)


def beside(left, right):
    return jnp.concatenate([left, right])


def scatter_first(parts):
    y_keep, y_send, x_keep, x_send = parts
    return scatter_first_sum(y_keep, over_y(y_send), x_keep, over_x(x_send))


def scatter_first_sum(y_keep, y_other, x_keep, x_other):
    rows = y_keep.shape[0] // 4
    left, left_send = [
        beside(*[add_low(y_keep[at:][:rows], y_other[at:][:rows]) for at in (start, start + 2 * rows)])
        for start in (0, rows)
    ]
    return (
        left,
        left_send,
        add_low(x_keep[: 2 * rows], x_other[: 2 * rows]),
        add_low(x_keep[2 * rows :], x_other[2 * rows :]),
    )


def scatter_second(parts):
    left, left_send, right, right_send = parts
    return add_low(left, over_x(left_send)), add_low(right, over_y(right_send))


def scatter_both(later, sooner):
    left, left_send, right, right_send = later
    y_keep, y_send, x_keep, x_send = sooner
    rows = left.shape[0]
    x_other = over_x(beside(left_send, x_send))
    y_other = over_y(beside(right_send, y_send))
    done = add_low(left, x_other[:rows]), add_low(right, y_other[:rows])
    return done, scatter_first_sum(y_keep, y_other[rows:], x_keep, x_other[rows:])


def scatter_near(parts):
    quarters = [part.reshape(2, 4, part.shape[0] // 8, -1) for part in parts]
    stack = [
        jnp.concatenate([half[core, step] for half in quarters for core in (0, 1)]) for step in range(4)
    ]
    terms = [stack[0]] + [over_z(stack[step], step) for step in (1, 2, 3)]
    terms = [term.astype(jnp.float32) for term in terms]
    return (terms[0] + terms[1]) + (terms[2] + terms[3])


def scatter_last(sums, core_index):
    rows = sums[0].shape[0] // 4
    split = [
        [jnp.concatenate([total[at:][:rows] for at in (core * rows, (core + 2) * rows)]) for core in (0, 1)]
        for total in sums
    ]
    other = over_core(jnp.concatenate([send for _, send in split], axis=1))
    width = sums[0].shape[1]
    pairs = []
    for index, (keep, _) in enumerate(split):
        there = other[:, index * width :][:, :width]
        pairs.append((jnp.where(core_index == 0, keep, there), jnp.where(core_index == 0, there, keep)))
    return pairs


def sum_chips(array):
    array = array + over_core(array)
    array = array + over_x(array)
    return array + over_y(array)


def sum_near(array):
    return (array + over_z(array, 1)) + (over_z(array, 2) + over_z(array, 3))


def head_scores(queries, key_rows, same_doc):
    raw_scores = outer_cols(queries * jnp.bfloat16(HEAD_DIM ** (-0.5)), key_rows)
    return jnp.where(same_doc, raw_scores, -1000000000.0)


def attend_forward_kernel(q_ref, k_ref, v_ref, column_ref, row_ref, ctx_ref, logsum_ref):
    lane = lax.broadcasted_iota(jnp.int32, q_ref.shape, 1) // HEAD_DIM
    same_doc = column_ref[...] == row_ref[...]
    value_rows = v_ref[...]
    contexts = []
    logsums = []
    for head in (0, 1):
        queries = jnp.where(lane == head, q_ref[...], jnp.bfloat16(0))
        scores = head_scores(queries, k_ref[...], same_doc)
        row_max = jnp.max(scores, axis=-1, keepdims=True)
        exponent = jnp.exp(scores - row_max)
        row_total = jnp.sum(exponent, axis=-1, keepdims=True)
        probabilities = (exponent * (1.0 / row_total)).astype(jnp.bfloat16)
        contexts.append(matmul(probabilities, value_rows))
        logsums.append(row_max + jnp.log(row_total))
    ctx_ref[...] = jnp.where(lane == 0, contexts[0], contexts[1]).astype(jnp.bfloat16)
    logsum_ref[...] = jnp.where(lane == 0, logsums[0], logsums[1])


def attend_backward_kernel(
    q_ref, k_ref, v_ref, column_ref, row_ref, logsum_ref, dctx_ref, out_ref
):
    lane = lax.broadcasted_iota(jnp.int32, q_ref.shape, 1) // HEAD_DIM
    same_doc = column_ref[...] == row_ref[...]
    key_rows = k_ref[...]
    value_rows = v_ref[...]
    results = []
    for head in (0, 1):
        queries = jnp.where(lane == head, q_ref[...], jnp.bfloat16(0))
        d_context = jnp.where(lane == head, dctx_ref[...], jnp.bfloat16(0))
        scores = head_scores(queries, key_rows, same_doc)
        place = head * HEAD_DIM
        probabilities = jnp.exp(scores - logsum_ref[:, place : place + 1])
        d_probs = outer_cols(d_context, value_rows)
        row_dot = jnp.sum(d_probs * probabilities, axis=-1, keepdims=True)
        d_raw = (probabilities * (d_probs - row_dot) * HEAD_DIM ** (-0.5)).astype(jnp.bfloat16)
        results.append(
            (
                matmul(d_raw, key_rows),
                inner_rows(d_raw, queries),
                inner_rows(probabilities.astype(jnp.bfloat16), d_context),
            )
        )
    pairs = pl.num_programs(1)
    first = pl.program_id(0) * 3 * pairs + pl.program_id(1)
    for part, (left, right) in enumerate(zip(*results)):
        place = pl.multiple_of((first + part * pairs) * 128, 128)
        out_ref[:, pl.ds(place, 128)] = jnp.where(lane == 0, left, right).astype(jnp.bfloat16)


def kernel_options():
    return dict(
        cost_estimate=pl.CostEstimate(flops=0, bytes_accessed=0, transcendentals=0),
        compiler_params=pltpu.CompilerParams(vmem_limit_bytes=32 << 20),
    )


def attention_inputs(rows, pairs, column, row):
    def place(part):
        return lambda group, pair: (0, group * 3 * pairs + part * pairs + pair)

    whole = lambda group, pair: (0, 0)
    return [pl.BlockSpec((rows, 128), place(part)) for part in range(3)] + [
        pl.BlockSpec(column.shape, whole),
        pl.BlockSpec(row.shape, whole),
    ]


def attend_rows_forward(qkv, column, row):
    rows, pairs = qkv.shape[0], qkv.shape[1] // 768
    own = pl.BlockSpec((rows, 128), lambda group, pair: (0, group * pairs + pair))
    return pl.pallas_call(
        attend_forward_kernel,
        grid=(2, pairs),
        in_specs=attention_inputs(rows, pairs, column, row),
        out_specs=[own, own],
        out_shape=[
            jax.ShapeDtypeStruct((rows, pairs * 256), jnp.bfloat16),
            jax.ShapeDtypeStruct((rows, pairs * 256), jnp.float32),
        ],
        **kernel_options(),
    )(qkv, qkv, qkv, column, row)


def attend_rows_backward(qkv, column, row, logsum, d_context):
    rows, pairs = qkv.shape[0], qkv.shape[1] // 768
    own = pl.BlockSpec((rows, 128), lambda group, pair: (0, group * pairs + pair))
    return pl.pallas_call(
        attend_backward_kernel,
        grid=(2, pairs),
        in_specs=attention_inputs(rows, pairs, column, row) + [own, own],
        out_specs=pl.BlockSpec(qkv.shape, lambda group, pair: (0, 0)),
        out_shape=jax.ShapeDtypeStruct(qkv.shape, jnp.bfloat16),
        **kernel_options(),
    )(qkv, qkv, qkv, column, row, logsum, d_context)


def weight_specs(weight, start, steps, step):
    rows = weight[0].shape[0]
    first = start // step
    left = pl.BlockSpec((rows, step), lambda group, at: (0, first + jnp.where(group == 0, at, steps - 1)))
    other = pl.BlockSpec((rows, step), lambda group, at: (0, first + jnp.where(group == 1, at, 0)))
    right = pl.BlockSpec((rows // 2, step), lambda group, at: (group, first + at))
    return [left, other, right, right] * 2


def with_block(refs, use):
    for group in (0, 1):

        @pl.when(pl.program_id(0) == group)
        def _():
            parts = (refs[group], refs[2], refs[3], refs[4 + group], refs[6], refs[7])
            use(jnp.concatenate([part[...] for part in parts], axis=0))


def expand_rows(rows, weight, start, width, step, finish, extras, out_types):
    count = len(weight)

    def kernel(rows_ref, *refs):
        def use(block):
            total = matmul(rows_ref[...], block)
            results = finish(total, *[ref[...] for ref in refs[count : count + len(extras)]])
            for ref, result in zip(refs[count + len(extras) :], results):
                ref[...] = result

        with_block(refs[:count], use)

    steps = width // step

    def own(height):
        return pl.BlockSpec((height, step), lambda group, at: (0, group * steps + at))

    return pl.pallas_call(
        kernel,
        grid=(2, steps),
        in_specs=[pl.BlockSpec(rows.shape, lambda group, at: (0, 0))]
        + weight_specs(weight, start, steps, step)
        + [own(extra.shape[0]) for extra in extras],
        out_specs=[own(height) for height, _ in out_types],
        out_shape=[jax.ShapeDtypeStruct((height, 2 * width), kind) for height, kind in out_types],
        **kernel_options(),
    )(rows, *weight, *extras)


def contract_rows(rows, weight, start, width, step):
    steps = width // step
    shape = (rows.shape[0], 4 * weight[0].shape[0])

    def kernel(rows_ref, *refs):
        out_ref = refs[-1]

        @pl.when((pl.program_id(0) == 0) & (pl.program_id(1) == 0))
        def _():
            out_ref[...] = jnp.zeros_like(out_ref)

        def use(block):
            out_ref[...] += outer_cols(rows_ref[...], block)

        with_block(refs[:-1], use)

    return pl.pallas_call(
        kernel,
        grid=(2, steps),
        in_specs=[pl.BlockSpec((rows.shape[0], step), lambda group, at: (0, group * steps + at))]
        + weight_specs(weight, start, steps, step),
        out_specs=pl.BlockSpec(shape, lambda group, at: (0, 0)),
        out_shape=jax.ShapeDtypeStruct(shape, jnp.float32),
        **kernel_options(),
    )(rows, *weight)


def grad_parts(terms):
    depth = terms[0][0].shape[1]
    half, quarter, eighth = depth // 2, depth // 4, depth // 8
    widths = [units.shape[1] // 2 for _, _, units, _ in terms]
    total_width = sum(widths)

    def kernel(*refs):
        y_keep, y_send, x_keep, x_send = refs[-4:]
        start = 0
        for index, width in enumerate(widths):
            rows, rows_other, units, units_other = refs[4 * index :][:4]
            columns = slice(start, start + width)
            start += width
            for core in (0, 1):
                here = slice(core * half, (core + 1) * half)
                there = slice((1 - core) * half, (2 - core) * half)
                total = inner_rows(rows[:, here], units[...])
                total = total + inner_rows(rows_other[:, there], units_other[...])
                total = total.astype(jnp.bfloat16)
                place = slice(core * quarter, (core + 1) * quarter)

                @pl.when(pl.program_id(0) == 0)
                def _():
                    y_keep[place, columns] = total[:quarter]

                @pl.when(pl.program_id(0) == 1)
                def _():
                    y_send[place, columns] = total[:quarter]

                place = slice(core * eighth, (core + 1) * eighth)
                x_keep[place, columns] = total[quarter : quarter + eighth]
                x_send[place, columns] = total[quarter + eighth :]

    in_specs = []
    for (rows, _, units, _), width in zip(terms, widths):
        whole = pl.BlockSpec(rows.shape, lambda group: (0, 0))
        own = pl.BlockSpec((units.shape[0], width), lambda group: (0, group))
        in_specs += [whole, whole, own, own]
    y_spec = pl.BlockSpec((half, total_width), lambda group: (0, 0))
    x_spec = pl.BlockSpec((quarter, total_width), lambda group: (group, 0))
    return pl.pallas_call(
        kernel,
        grid=(2,),
        in_specs=in_specs,
        out_specs=[y_spec, y_spec, x_spec, x_spec],
        out_shape=[jax.ShapeDtypeStruct((half, total_width), jnp.bfloat16)] * 4,
        **kernel_options(),
    )(*[array for term in terms for array in term])


def gelu_pair(inputs):
    share = 0.5 * (1.0 + lax.erf(inputs * 0.5**0.5))
    slope = share + inputs * (jnp.exp(-0.5 * inputs * inputs) * (0.5 / jnp.pi) ** 0.5)
    return (inputs * share).astype(jnp.bfloat16), slope.astype(jnp.bfloat16)


def data_plan(
    tokens,
    segments,
    w_qkv,
    bias_qv,
    w_out,
    bias_out,
    ln1_gain,
    ln1_bias,
    w_up,
    bias_up,
    w_down,
    bias_down,
    ln2_gain,
    ln2_bias,
    d_out,
):
    low, wide = jnp.bfloat16, jnp.float32
    dp_index = lax.axis_index("dp")
    tensor_index = lax.axis_index("tensor")
    width = tokens.shape[1]
    head_width = w_qkv.shape[2]
    unit_width = w_up.shape[1]
    groups = (0, 1)

    place = jnp.arange(width)
    block = ((place // 32) % 4) * 4 + ((place // 128) % 2) * 2 + place // 512
    source = (dp_index ^ block) * 64 + ((place // 256) % 2) * 32 + place % 32
    order = (jnp.arange(width)[:, None] == source[None, :]).astype(low)

    def group_of(vector, group, size):
        return lax.dynamic_slice_in_dim(vector, (tensor_index ^ group) * size, size, axis=-1)

    def whole_of(parts):
        left, right = parts
        return jnp.where(
            tensor_index == 0,
            jnp.concatenate([left, right], axis=-1),
            jnp.concatenate([right, left], axis=-1),
        )

    vectors = jnp.dot(
        jnp.stack([bias_out, ln1_gain, ln1_bias, bias_down, ln2_gain, ln2_bias]),
        order.astype(wide),
        precision=lax.Precision.HIGHEST,
    )
    bias_out, ln1_gain, ln1_bias, bias_down, ln2_gain, ln2_bias = [vectors[i] for i in range(6)]
    own_rows = matmul(tokens, order).astype(low)
    cotangent = matmul(d_out, order)

    which = lax.dynamic_slice_in_dim(segments, tensor_index, 1, axis=0)
    column, row = which.reshape(SEQ, 1), which

    rows = tokens.shape[0]
    blank = jnp.zeros((head_width,), wide)
    qkv_bias = jnp.concatenate(
        [
            vector
            for group in groups
            for vector in (
                group_of(bias_qv[0], group, head_width),
                blank,
                group_of(bias_qv[1], group, head_width),
            )
        ]
    )[None]
    units_bias = jnp.concatenate([group_of(bias_up, group, unit_width) for group in groups])[None]

    def attention_work(weight):
        (qkv,) = expand_rows(
            own_rows,
            weight,
            0,
            3 * head_width,
            3 * head_width // 2,
            lambda total, bias: ((total + bias).astype(low),),
            [qkv_bias],
            [(rows, low)],
        )
        context, logsum = attend_rows_forward(qkv, column, row)
        return dict(qkv=qkv, context=context, logsum=logsum)

    def units_work(weight, results):
        attn_rows = contract_rows(results["context"], weight, unit_width, head_width, head_width)
        z_one = own_rows.astype(wide) + attn_rows + bias_out
        h_one, scaled_one, spread_one = norm_forward(z_one, ln1_gain, ln1_bias)
        h_low = h_one.astype(low)
        activation, slope = expand_rows(
            h_low,
            weight,
            0,
            unit_width,
            unit_width // 4,
            lambda total, bias: gelu_pair(total + bias),
            [units_bias],
            [(rows, low), (rows, low)],
        )
        return results | dict(
            norm=(h_one, scaled_one, spread_one), h_low=h_low, activation=activation, slope=slope
        )

    (qkv_w, up_out_w, down_w), made = gather_weights(
        [
            jnp.concatenate([w_qkv[0], w_qkv[1], w_qkv[2]], axis=1),
            jnp.concatenate([w_up, w_out.T], axis=1),
            w_down.T,
        ],
        attention_work,
        units_work,
    )
    qkv, context, logsum = made["qkv"], made["context"], made["logsum"]
    h_one, scaled_one, spread_one = made["norm"]
    h_low, activation, slope = made["h_low"], made["activation"], made["slope"]
    mlp_rows = contract_rows(activation, down_w, 0, unit_width, unit_width // 2)
    z_two = h_one + mlp_rows + bias_down
    normed, scaled_two, spread_two = norm_forward(z_two, ln2_gain, ln2_bias)
    output = outer_cols(normed.astype(low), order).astype(low)

    grad_two, d_gain_two, d_offset_two = norm_backward(cotangent, scaled_two, spread_two, ln2_gain)
    d_bias_down = jnp.sum(grad_two, axis=0)
    grad_two_low = grad_two.astype(low)

    after = lax.optimization_barrier
    core_index = dp_index % 2

    def core_halves(units, parts):
        size = units.shape[1] // (4 * parts)
        return [
            jnp.concatenate(
                [
                    lax.dynamic_slice_in_dim(units, 2 * size * at + core * size, size, axis=1)
                    for at in range(2 * parts)
                ],
                axis=1,
            )
            for core in (core_index, 1 - core_index)
        ]

    act_own, act_send = core_halves(activation, 1)
    grad_two_low, slope, act_own, act_send = after((grad_two_low, slope, act_own, act_send))
    grad_two_other, act_other = over_core(grad_two_low), over_core(act_send)

    def finish_units(total, slope):
        units = (total * slope.astype(wide)).astype(low)
        return units, jnp.sum(units.astype(wide), axis=0, keepdims=True)

    d_up, d_bias_units = expand_rows(
        grad_two_low,
        down_w,
        0,
        unit_width,
        unit_width // 2,
        finish_units,
        [slope],
        [(rows, low), (1, wide)],
    )
    up_own, up_send = core_halves(d_up, 1)
    context_own, context_send = core_halves(context, 1)
    (grad_two_other, act_other, d_up, up_own, up_send, h_low, own_rows, context_own, context_send) = after(
        (grad_two_other, act_other, d_up, up_own, up_send, h_low, own_rows, context_own, context_send)
    )
    up_other, h_other = over_core(up_send), over_core(h_low)
    rows_other, context_other = over_core(own_rows), over_core(context_send)
    down_sum = grad_parts([(grad_two_low, grad_two_other, act_own, act_other)])
    down_sum, up_other, h_other, rows_other, context_other, d_up = after(
        (down_sum, up_other, h_other, rows_other, context_other, d_up)
    )
    down_sum = scatter_first(down_sum)
    mlp_back = contract_rows(d_up, up_out_w, 0, unit_width, unit_width // 2)
    grad_one, d_gain_one, d_offset_one = norm_backward(
        mlp_back + grad_two, scaled_one, spread_one, ln1_gain
    )
    d_bias_out = jnp.sum(grad_one, axis=0)
    grad_one_low = grad_one.astype(low)
    up_sum = grad_parts([(h_low, h_other, up_own, up_other)])
    (d_ctx,) = expand_rows(
        grad_one_low,
        up_out_w,
        unit_width,
        head_width,
        head_width,
        lambda total: (total.astype(low),),
        [],
        [(rows, low)],
    )
    down_sum, up_sum, d_ctx, grad_one_low = after((down_sum, up_sum, d_ctx, grad_one_low))
    down_sum, up_sum = scatter_both(down_sum, up_sum)
    grad_one_other = over_core(grad_one_low)
    d_qkv = attend_rows_backward(qkv, column, row, logsum, d_ctx)
    qkv_own, qkv_send = core_halves(d_qkv, 3)
    qkv_other = over_core(qkv_send)
    last_sum = grad_parts(
        [
            (own_rows, rows_other, qkv_own, qkv_other),
            (grad_one_low, grad_one_other, context_own, context_other),
        ]
    )
    down_sum, up_sum, last_sum, d_qkv = after((down_sum, up_sum, last_sum, d_qkv))
    up_sum, last_sum = scatter_both(up_sum, last_sum)
    down_sum = scatter_near(down_sum)
    attn_back = contract_rows(d_qkv, qkv_w, 0, 3 * head_width, 3 * head_width // 2)
    grad_rows = attn_back + grad_one
    upper = grad_rows.astype(low)
    lower = (grad_rows - upper.astype(wide)).astype(low)
    grad_tokens = outer_cols(upper, order) + outer_cols(lower, order)
    d_bias_up = whole_of([d_bias_units[0, :unit_width], d_bias_units[0, unit_width:]])
    sums = jnp.sum(d_qkv, axis=0, dtype=wide).reshape(2, 3, head_width)
    d_bias_q = whole_of([sums[0, 0], sums[1, 0]])
    d_bias_v = whole_of([sums[0, 2], sums[1, 2]])
    narrow = jnp.dot(
        jnp.stack([d_bias_out, d_gain_one, d_offset_one, d_bias_down, d_gain_two, d_offset_two]),
        order.astype(wide).T,
        precision=lax.Precision.HIGHEST,
    )
    small = jnp.concatenate(
        [narrow, d_bias_q[None], d_bias_v[None], d_bias_up.reshape(-1, width)], axis=0
    )
    down_sum, up_sum, last_sum = after((down_sum, up_sum, last_sum))
    up_sum = scatter_near(up_sum)
    last_sum = scatter_second(last_sum)
    up_sum, last_sum, small = after((up_sum, last_sum, small))
    last_sum = scatter_near(last_sum)
    small = sum_chips(small)
    last_sum, small = after((last_sum, small))
    small = sum_near(small)
    pairs = scatter_last([down_sum, up_sum, last_sum], core_index)
    grad_w_down = jnp.concatenate(pairs[0], axis=1).T
    grad_w_up = jnp.concatenate(pairs[1], axis=1)
    size = head_width // 2
    parts = [
        jnp.concatenate([part[:, at * size :][:, :size] for part in pairs[2]], axis=1) for at in range(4)
    ]
    grad_w_qkv = jnp.stack(parts[:3])
    grad_w_out = parts[3].T

    return (
        output,
        grad_tokens,
        grad_w_qkv,
        small[6:8],
        grad_w_out,
        small[0],
        small[1],
        small[2],
        grad_w_up,
        small[8:].reshape(-1),
        grad_w_down,
        small[3],
        small[4],
        small[5],
    )


def local(*arrays):
    tokens = arrays[0]
    sizes = (lax.axis_size("dp"), lax.axis_size("tensor"))
    if sizes == (16, 2) and tokens.shape == (SEQ, 1024):
        return data_plan(*arrays)
    return tensor_plan(*arrays)


def solution(mesh):
    return jax.shard_map(
        local,
        mesh=mesh,
        in_specs=(
            P(("dp", "tensor"), None),
            P("dp", None),
            P(None, "dp", "tensor"),
            P(),
            P("tensor", "dp"),
            P(),
            P(),
            P(),
            P("dp", "tensor"),
            P(),
            P("tensor", "dp"),
            P(),
            P(),
            P(),
            P(("dp", "tensor"), None),
        ),
        out_specs=(
            P(("dp", "tensor"), None),
            P(("dp", "tensor"), None),
            P(None, "dp", "tensor"),
            P(),
            P("tensor", "dp"),
            P(),
            P(),
            P(),
            P("dp", "tensor"),
            P(),
            P("tensor", "dp"),
            P(),
            P(),
            P(),
        ),
        check_vma=False,
    )
```

```python
import functools

import jax
import jax.numpy as jnp
from jax import lax
from jax.experimental import pallas as pl
from jax.experimental.pallas import tpu as pltpu
from jax.sharding import PartitionSpec as P

HEAD_DIM = 64
SEQ = 512


eps = 1e-12


def matmul(left, right):
    return jnp.dot(left, right, preferred_element_type=jnp.float32)


def inner_rows(left, right):
    return lax.dot_general(
        left, right, (((0,), (0,)), ((), ())), preferred_element_type=jnp.float32
    )


def outer_cols(left, right):
    return lax.dot_general(
        left, right, (((1,), (1,)), ((), ())), preferred_element_type=jnp.float32
    )


def norm_forward(inputs, gain_vec, offset):
    center = jnp.mean(inputs, axis=-1, keepdims=True)
    spread = lax.rsqrt(jnp.mean(jnp.square(inputs - center), axis=-1, keepdims=True) + eps)
    scaled = (inputs - center) * spread
    return (scaled * gain_vec + offset, scaled, spread)


def norm_backward(gradient, scaled, spread, gain_vec):
    d_gain = jnp.sum(gradient * scaled, axis=0)
    d_offset = jnp.sum(gradient, axis=0)
    d_scaled = gradient * gain_vec
    d_inputs = spread * (
        d_scaled
        - jnp.mean(d_scaled, axis=-1, keepdims=True)
        - scaled * jnp.mean(d_scaled * scaled, axis=-1, keepdims=True)
    )
    return (d_inputs, d_gain, d_offset)


def masked_scores(queries, key_rows, segment):
    raw_scores = jnp.einsum("qhd,khd->hqk", queries, key_rows, preferred_element_type=jnp.float32)
    same_doc = segment[:, None] == segment[None, :]
    return jnp.where(same_doc[None], raw_scores * HEAD_DIM ** (-0.5), -1000000000.0)


def attend_forward(block):
    queries, key_rows, value_rows, segment = block
    scores = masked_scores(queries, key_rows, segment)
    row_max = jnp.max(scores, axis=-1, keepdims=True)
    exponent = jnp.exp(scores - row_max)
    row_total = jnp.sum(exponent, axis=-1, keepdims=True)
    probabilities = (exponent / row_total).astype(jnp.bfloat16)
    context = jnp.einsum(
        "hqk,khd->qhd", probabilities, value_rows, preferred_element_type=jnp.float32
    )
    return (context.astype(jnp.bfloat16), row_max[..., 0] + jnp.log(row_total[..., 0]))


def attend_backward(block):
    queries, key_rows, value_rows, segment, logsum, d_context = block
    scores = masked_scores(queries, key_rows, segment)
    probabilities = jnp.exp(scores - logsum[..., None])
    d_probs = jnp.einsum("qhd,khd->hqk", d_context, value_rows, preferred_element_type=jnp.float32)
    row_dot = jnp.sum(d_probs * probabilities, axis=-1, keepdims=True)
    d_raw = (probabilities * (d_probs - row_dot) * HEAD_DIM ** (-0.5)).astype(jnp.bfloat16)
    d_queries = jnp.einsum("hqk,khd->qhd", d_raw, key_rows, preferred_element_type=jnp.float32)
    d_keys = jnp.einsum("hqk,qhd->khd", d_raw, queries, preferred_element_type=jnp.float32)
    d_values = jnp.einsum(
        "hqk,qhd->khd",
        probabilities.astype(jnp.bfloat16),
        d_context,
        preferred_element_type=jnp.float32,
    )
    return (
        d_queries.astype(jnp.bfloat16),
        d_keys.astype(jnp.bfloat16),
        d_values.astype(jnp.bfloat16),
    )


def tensor_plan(
    tokens,
    segments,
    w_qkv,
    bias_qv,
    w_out,
    bias_out,
    ln1_gain,
    ln1_bias,
    w_up,
    bias_up,
    w_down,
    bias_down,
    ln2_gain,
    ln2_bias,
    d_out,
):
    qkv_w, out_w, up_w, down_w = (
        lax.all_gather(w_qkv, "dp", axis=1, tiled=True),
        lax.all_gather(w_out, "dp", axis=1, tiled=True),
        lax.all_gather(w_up, "dp", axis=0, tiled=True),
        lax.all_gather(w_down, "dp", axis=1, tiled=True),
    )
    head_width = qkv_w.shape[2]
    unit_width = up_w.shape[1]
    tensor_index = lax.axis_index("tensor")
    bias_query = lax.dynamic_slice_in_dim(bias_qv[0], tensor_index * head_width, head_width)
    bias_value = lax.dynamic_slice_in_dim(bias_qv[1], tensor_index * head_width, head_width)
    bias_units = lax.dynamic_slice_in_dim(bias_up, tensor_index * unit_width, unit_width)
    block_rows = lax.all_gather(tokens, "tensor", axis=0, tiled=True)
    pieces = [
        matmul(block_rows, qkv_w[0]) + bias_query,
        matmul(block_rows, qkv_w[1]),
        matmul(block_rows, qkv_w[2]) + bias_value,
    ]
    qkv_all = jnp.concatenate(pieces, axis=1)
    qkv_rows = qkv_all.astype(jnp.bfloat16)
    group_rows = qkv_rows.shape[0]
    shape_seq = (segments.shape[0], SEQ, head_width // HEAD_DIM, HEAD_DIM)
    queries = qkv_rows[:, :head_width].reshape(shape_seq)
    key_rows = qkv_rows[:, head_width : 2 * head_width].reshape(shape_seq)
    value_rows = qkv_rows[:, 2 * head_width :].reshape(shape_seq)
    context, logsum = lax.map(attend_forward, (queries, key_rows, value_rows, segments))
    context_rows = context.reshape(group_rows, head_width)
    attn_rows = lax.psum_scatter(
        matmul(context_rows, out_w).astype(jnp.bfloat16), "tensor", scatter_dimension=0, tiled=True
    ).astype(jnp.float32)
    z_one = tokens.astype(jnp.float32) + attn_rows + bias_out
    h_one, scaled_one, spread_one = norm_forward(z_one, ln1_gain, ln1_bias)
    h_low = h_one.astype(jnp.bfloat16)
    pieces = [matmul(lax.all_gather(h_low, "tensor", axis=0, tiled=True), up_w) + bias_units]
    up_all = pieces[0]
    activation = jax.nn.gelu(up_all, approximate=False).astype(jnp.bfloat16)
    mlp_rows = lax.psum_scatter(
        matmul(activation, down_w).astype(jnp.bfloat16), "tensor", scatter_dimension=0, tiled=True
    ).astype(jnp.float32)
    z_two = h_one + mlp_rows + bias_down
    normed, scaled_two, spread_two = norm_forward(z_two, ln2_gain, ln2_bias)
    output = normed.astype(jnp.bfloat16)
    qkv_w, out_w, up_w, down_w = (
        lax.all_gather(w_qkv, "dp", axis=1, tiled=True),
        lax.all_gather(w_out, "dp", axis=1, tiled=True),
        lax.all_gather(w_up, "dp", axis=0, tiled=True),
        lax.all_gather(w_down, "dp", axis=1, tiled=True),
    )
    grad_two, d_gain_two, d_offset_two = norm_backward(
        d_out.astype(jnp.float32), scaled_two, spread_two, ln2_gain
    )
    d_bias_down = jnp.sum(grad_two, axis=0)
    grad_two_low = grad_two.astype(jnp.bfloat16)
    block_rows = lax.all_gather(grad_two_low, "tensor", axis=0, tiled=True)
    d_act = outer_cols(block_rows, down_w)
    d_wdown, d_act = (inner_rows(activation, block_rows), d_act)
    gelu_pull = jax.vjp(lambda inputs: jax.nn.gelu(inputs, approximate=False), up_all)[1]
    d_up = gelu_pull(d_act)[0].astype(jnp.bfloat16)
    d_bias_units = jnp.sum(d_up, axis=0, dtype=jnp.float32)
    d_bias_up = lax.dynamic_update_slice_in_dim(
        jnp.zeros(bias_up.shape, jnp.float32), d_bias_units, tensor_index * unit_width, 0
    )
    mlp_back = lax.psum_scatter(
        outer_cols(d_up, up_w).astype(jnp.bfloat16), "tensor", scatter_dimension=0, tiled=True
    ).astype(jnp.float32)
    d_wup = inner_rows(lax.all_gather(h_low, "tensor", axis=0, tiled=True), d_up)
    grad_one, d_gain_one, d_offset_one = norm_backward(
        mlp_back + grad_two, scaled_one, spread_one, ln1_gain
    )
    d_bias_out = jnp.sum(grad_one, axis=0)
    grad_one_low = grad_one.astype(jnp.bfloat16)
    block_rows = lax.all_gather(grad_one_low, "tensor", axis=0, tiled=True)
    d_ctx = outer_cols(block_rows, out_w)
    d_wout, d_ctx = (inner_rows(context_rows, block_rows), d_ctx)
    d_ctx_low = d_ctx.astype(jnp.bfloat16).reshape(shape_seq)
    d_queries, d_keys, d_values = lax.map(
        attend_backward, (queries, key_rows, value_rows, segments, logsum, d_ctx_low)
    )
    d_qkv = jnp.concatenate(
        [
            d_queries.reshape(group_rows, head_width),
            d_keys.reshape(group_rows, head_width),
            d_values.reshape(group_rows, head_width),
        ],
        axis=1,
    )
    bias_pair = jnp.stack(
        [
            jnp.sum(d_qkv[:, :head_width], axis=0, dtype=jnp.float32),
            jnp.sum(d_qkv[:, 2 * head_width :], axis=0, dtype=jnp.float32),
        ]
    )
    d_bias_qv = lax.dynamic_update_slice_in_dim(
        jnp.zeros(bias_qv.shape, jnp.float32), bias_pair, tensor_index * head_width, 1
    )
    total_rows = outer_cols(d_qkv[:, :head_width], qkv_w[0])
    total_rows = total_rows + outer_cols(d_qkv[:, head_width : 2 * head_width], qkv_w[1])
    attn_back = lax.psum_scatter(
        (total_rows + outer_cols(d_qkv[:, 2 * head_width :], qkv_w[2])).astype(jnp.bfloat16),
        "tensor",
        scatter_dimension=0,
        tiled=True,
    ).astype(jnp.float32)
    grad_tokens = attn_back + grad_one
    block_rows = lax.all_gather(tokens, "tensor", axis=0, tiled=True)
    grads_part = d_qkv
    grads_part = grads_part.reshape(block_rows.shape[0], 3, head_width)
    d_wqkv = jnp.einsum("rd,rtc->tdc", block_rows, grads_part, preferred_element_type=jnp.float32)
    grad_w_qkv, grad_w_out, grad_w_up, grad_w_down = (
        lax.psum_scatter(d_wqkv.astype(jnp.bfloat16), "dp", scatter_dimension=1, tiled=True).astype(
            jnp.float32
        ),
        lax.psum_scatter(d_wout.astype(jnp.bfloat16), "dp", scatter_dimension=1, tiled=True).astype(
            jnp.float32
        ),
        lax.psum_scatter(d_wup.astype(jnp.bfloat16), "dp", scatter_dimension=0, tiled=True).astype(
            jnp.float32
        ),
        lax.psum_scatter(
            d_wdown.astype(jnp.bfloat16), "dp", scatter_dimension=1, tiled=True
        ).astype(jnp.float32),
    )
    small_grads = lax.psum(
        (
            d_bias_qv,
            d_bias_out,
            d_gain_one,
            d_offset_one,
            d_bias_up,
            d_bias_down,
            d_gain_two,
            d_offset_two,
        ),
        ("dp", "tensor"),
    )
    return (
        output,
        grad_tokens,
        grad_w_qkv,
        small_grads[0],
        grad_w_out,
        small_grads[1],
        small_grads[2],
        small_grads[3],
        grad_w_up,
        small_grads[4],
        grad_w_down,
        small_grads[5],
        small_grads[6],
        small_grads[7],
    )


def swap(array, name, mask):
    size = lax.axis_size(name)
    return lax.ppermute(array, name, [(index, index ^ mask) for index in range(size)])


def over_y(array):
    return swap(array, "tensor", 1)


def over_x(array):
    return swap(array, "dp", 2)


def over_core(array):
    return swap(array, "dp", 1)


def over_z(array, step):
    return swap(array, "dp", 4 * step)


def gather_first(stack):
    rows = stack[0].shape[0] // 2
    left, right = [jnp.concatenate([part[half * rows :][:rows] for part in stack]) for half in (0, 1)]
    return left, over_x(left), right, over_y(right)


def gather_second(parts):
    left = jnp.concatenate(parts[:2])
    right = jnp.concatenate(parts[2:])
    return left, over_y(left), right, over_x(right), over_core(left), over_core(right)


def gather_last(parts):
    left, left_other, right, right_other, left_core, right_core = parts
    here = (left, left_other, right, right_other)
    return here + (left_core, over_core(left_other), right_core, over_core(right_other))


def gather_weights(shards, first_work, second_work):
    after = lax.optimization_barrier
    one, two, three = shards
    one = [one] + [over_z(one, step) for step in (1, 2, 3)]
    two = [two, over_z(two, 1)]
    one, two, three = after((one, two, three))
    one = gather_first(one)
    two = two + [over_z(two[0], 2)]
    three = [three, over_z(three, 1)]
    one, two, three = after((one, two, three))
    one = gather_second(one)
    two = two + [over_z(two[1], 2)]
    one, two, three = after((one, two, three))
    two = gather_first(two)
    one = gather_last(one)
    three = three + [over_z(three[0], 2)]
    one, two, three = after((one, two, three))
    two = gather_second(two)
    three = three + [over_z(three[1], 2)]
    made = first_work(one)
    two, three, made = after((two, three, made))
    three = gather_first(three)
    two = gather_last(two)
    two, three, made = after((two, three, made))
    three = gather_second(three)
    made = second_work(two, made)
    three, made = after((three, made))
    return (one, two, gather_last(three)), made


def add_low(left, right):
    return (left.astype(jnp.float32) + right.astype(jnp.float32)).astype(jnp.bfloat16)


def beside(left, right):
    return jnp.concatenate([left, right])


def scatter_first(parts):
    y_keep, y_send, x_keep, x_send = parts
    return scatter_first_sum(y_keep, over_y(y_send), x_keep, over_x(x_send))


def scatter_first_sum(y_keep, y_other, x_keep, x_other):
    rows = y_keep.shape[0] // 4
    left, left_send = [
        beside(*[add_low(y_keep[at:][:rows], y_other[at:][:rows]) for at in (start, start + 2 * rows)])
        for start in (0, rows)
    ]
    return (
        left,
        left_send,
        add_low(x_keep[: 2 * rows], x_other[: 2 * rows]),
        add_low(x_keep[2 * rows :], x_other[2 * rows :]),
    )


def scatter_second(parts):
    left, left_send, right, right_send = parts
    return add_low(left, over_x(left_send)), add_low(right, over_y(right_send))


def scatter_both(later, sooner):
    left, left_send, right, right_send = later
    y_keep, y_send, x_keep, x_send = sooner
    rows = left.shape[0]
    x_other = over_x(beside(left_send, x_send))
    y_other = over_y(beside(right_send, y_send))
    done = add_low(left, x_other[:rows]), add_low(right, y_other[:rows])
    return done, scatter_first_sum(y_keep, y_other[rows:], x_keep, x_other[rows:])


def scatter_near(parts):
    quarters = [part.reshape(2, 4, part.shape[0] // 8, -1) for part in parts]
    stack = [
        jnp.concatenate([half[core, step] for half in quarters for core in (0, 1)]) for step in range(4)
    ]
    terms = [stack[0]] + [over_z(stack[step], step) for step in (1, 2, 3)]
    terms = [term.astype(jnp.float32) for term in terms]
    return (terms[0] + terms[1]) + (terms[2] + terms[3])


def scatter_last(sums, core_index):
    rows = sums[0].shape[0] // 4
    split = [
        [jnp.concatenate([total[at:][:rows] for at in (core * rows, (core + 2) * rows)]) for core in (0, 1)]
        for total in sums
    ]
    other = over_core(jnp.concatenate([send for _, send in split], axis=1))
    width = sums[0].shape[1]
    pairs = []
    for index, (keep, _) in enumerate(split):
        there = other[:, index * width :][:, :width]
        pairs.append((jnp.where(core_index == 0, keep, there), jnp.where(core_index == 0, there, keep)))
    return pairs


def sum_chips(array):
    array = array + over_core(array)
    array = array + over_x(array)
    return array + over_y(array)


def sum_near(array):
    return (array + over_z(array, 1)) + (over_z(array, 2) + over_z(array, 3))


def head_scores(queries, key_rows, same_doc):
    raw_scores = outer_cols(queries * jnp.bfloat16(HEAD_DIM ** (-0.5)), key_rows)
    return jnp.where(same_doc, raw_scores, -1000000000.0)


def attend_forward_kernel(
    core_ref, q_ref, k_ref, v_ref, column_ref, row_ref, own_ref, send_ref, logsum_ref
):
    lane = lax.broadcasted_iota(jnp.int32, q_ref.shape, 1) // HEAD_DIM
    same_doc = column_ref[...] == row_ref[...]
    value_rows = v_ref[...]
    contexts = []
    logsums = []
    for head in (0, 1):
        queries = jnp.where(lane == head, q_ref[...], jnp.bfloat16(0))
        scores = head_scores(queries, k_ref[...], same_doc)
        row_max = jnp.max(scores, axis=-1, keepdims=True)
        exponent = jnp.exp(scores - row_max)
        row_total = jnp.sum(exponent, axis=-1, keepdims=True)
        probabilities = (exponent * (1.0 / row_total)).astype(jnp.bfloat16)
        contexts.append(matmul(probabilities, value_rows))
        logsums.append(row_max + jnp.log(row_total))
    context = jnp.where(lane == 0, contexts[0], contexts[1]).astype(jnp.bfloat16)
    own = pl.program_id(1) < pl.num_programs(1) // 2

    @pl.when(own)
    def _():
        own_ref[...] = context

    @pl.when(jnp.logical_not(own))
    def _():
        send_ref[...] = context

    logsum_ref[...] = jnp.where(lane == 0, logsums[0], logsums[1])


def attend_backward_kernel(
    core_ref,
    q_ref,
    k_ref,
    v_ref,
    column_ref,
    row_ref,
    logsum_ref,
    dctx_ref,
    own_ref,
    send_ref,
    own_sum_ref,
    send_sum_ref,
):
    lane = lax.broadcasted_iota(jnp.int32, q_ref.shape, 1) // HEAD_DIM
    same_doc = column_ref[...] == row_ref[...]
    key_rows = k_ref[...]
    value_rows = v_ref[...]
    results = []
    for head in (0, 1):
        queries = jnp.where(lane == head, q_ref[...], jnp.bfloat16(0))
        d_context = jnp.where(lane == head, dctx_ref[...], jnp.bfloat16(0))
        scores = head_scores(queries, key_rows, same_doc)
        place = head * HEAD_DIM
        probabilities = jnp.exp(scores - logsum_ref[:, place : place + 1])
        d_probs = outer_cols(d_context, value_rows)
        row_dot = jnp.sum(d_probs * probabilities, axis=-1, keepdims=True)
        d_raw = (probabilities * (d_probs - row_dot) * HEAD_DIM ** (-0.5)).astype(jnp.bfloat16)
        results.append(
            (
                matmul(d_raw, key_rows),
                inner_rows(d_raw, queries),
                inner_rows(probabilities.astype(jnp.bfloat16), d_context),
            )
        )
    half = pl.num_programs(1) // 2
    at = pl.program_id(1)
    own = at < half
    first = pl.program_id(0) * 3 * half + jnp.where(own, at, at - half)
    for part, (left, right) in enumerate(zip(*results)):
        place = pl.ds(pl.multiple_of((first + part * half) * 128, 128), 128)
        gradient = jnp.where(lane == 0, left, right).astype(jnp.bfloat16)

        total = jnp.sum(gradient.astype(jnp.float32), axis=0, keepdims=True)

        @pl.when(own)
        def _():
            own_ref[:, place] = gradient
            own_sum_ref[:, place] = total

        @pl.when(jnp.logical_not(own))
        def _():
            send_ref[:, place] = gradient
            send_sum_ref[:, place] = total


def kernel_options(mebibytes):
    return dict(
        cost_estimate=pl.CostEstimate(flops=0, bytes_accessed=0, transcendentals=0),
        compiler_params=pltpu.CompilerParams(vmem_limit_bytes=mebibytes << 20),
    )


def call_kernel(
    kernel, core, mebibytes, grid, in_specs, out_specs, out_shape, operands, scratch_shapes=()
):
    return pl.pallas_call(
        kernel,
        grid_spec=pltpu.PrefetchScalarGridSpec(
            num_scalar_prefetch=1,
            grid=grid,
            in_specs=in_specs,
            out_specs=out_specs,
            scratch_shapes=scratch_shapes,
        ),
        out_shape=out_shape,
        **kernel_options(mebibytes),
    )(core, *operands)


def attention_inputs(rows, pairs, column, row):
    def place(part):
        return lambda group, at, core: (
            0,
            group * 3 * pairs + part * pairs + (at ^ (core[0] * (pairs // 2))),
        )

    whole = lambda group, at, core: (0, 0)
    return [pl.BlockSpec((rows, 128), place(part)) for part in range(3)] + [
        pl.BlockSpec(column.shape, whole),
        pl.BlockSpec(row.shape, whole),
    ]


def attend_rows_forward(core, qkv, column, row):
    rows, pairs = qkv.shape[0], qkv.shape[1] // 768
    half = pairs // 2
    own = pl.BlockSpec((rows, 128), lambda group, at, core: (0, group * half + jnp.minimum(at, half - 1)))
    send = pl.BlockSpec((rows, 128), lambda group, at, core: (0, group * half + jnp.maximum(at - half, 0)))
    flat = pl.BlockSpec((rows, 128), lambda group, at, core: (0, group * pairs + at))
    pair_shape = jax.ShapeDtypeStruct((rows, pairs * 128), jnp.bfloat16)
    own, send, logsum = call_kernel(
        attend_forward_kernel,
        core,
        16,
        (2, pairs),
        attention_inputs(rows, pairs, column, row),
        [own, send, flat],
        [pair_shape, pair_shape, jax.ShapeDtypeStruct((rows, pairs * 256), jnp.float32)],
        (qkv, qkv, qkv, column, row),
    )
    return (own, send), logsum


def attend_rows_backward(core, qkv, column, row, logsum, d_context):
    rows, pairs = qkv.shape[0], qkv.shape[1] // 768
    flat = pl.BlockSpec((rows, 128), lambda group, at, core: (0, group * pairs + at))
    pair_spec = pl.BlockSpec((rows, qkv.shape[1] // 2), lambda group, at, core: (0, 0))
    pair_shape = jax.ShapeDtypeStruct((rows, qkv.shape[1] // 2), jnp.bfloat16)
    sum_spec = pl.BlockSpec((1, qkv.shape[1] // 2), lambda group, at, core: (0, 0))
    sum_shape = jax.ShapeDtypeStruct((1, qkv.shape[1] // 2), jnp.float32)
    own, send, own_sum, send_sum = call_kernel(
        attend_backward_kernel,
        core,
        20,
        (2, pairs),
        attention_inputs(rows, pairs, column, row) + [flat, flat],
        [pair_spec, pair_spec, sum_spec, sum_spec],
        [pair_shape, pair_shape, sum_shape, sum_shape],
        (qkv, qkv, qkv, column, row, logsum, d_context),
    )
    return (own, send), (own_sum, send_sum)


def weight_specs(weight, start, parts, step):
    rows = weight[0].shape[0]
    first, last = start // step, 2 * parts - 1

    def column(at, core):
        return first + (at ^ core[0])

    left = pl.BlockSpec(
        (rows, step), lambda group, at, core: (0, column(jnp.where(group == 0, at, last), core))
    )
    other = pl.BlockSpec(
        (rows, step), lambda group, at, core: (0, column(jnp.where(group == 1, at, 0), core))
    )
    right = pl.BlockSpec((rows // 2, step), lambda group, at, core: (group, column(at, core)))
    return [left, other, right, right] * 2


def load_block(refs, block_ref):
    for group in (0, 1):

        @pl.when(pl.program_id(0) == group)
        def _():
            start = 0
            for part in (refs[group], refs[2], refs[3], refs[4 + group], refs[6], refs[7]):
                block_ref[start : start + part.shape[0], :] = part[...]
                start += part.shape[0]


def pair_specs(height, parts, step):
    return [pl.BlockSpec((height, step), lambda group, at, core: (0, group * parts + at // 2))] * 2


def expand_rows(core, rows, weight, start, width, parts, finish, extras, out_types):
    step = width // (2 * parts)
    in_specs = [pl.BlockSpec(rows.shape, lambda group, at, core: (0, 0))]
    in_specs += weight_specs(weight, start, parts, step)
    operands = [rows, *weight]
    for extra in extras:
        if isinstance(extra, tuple):
            in_specs += pair_specs(extra[0].shape[0], parts, step)
            operands += extra
        else:
            in_specs.append(
                pl.BlockSpec((1, step), lambda group, at, core: (0, group * 2 * parts + (at ^ core[0])))
            )
            operands.append(extra)
    out_specs, out_shape = [], []
    for height, kind, paired in out_types:
        if paired:
            out_specs += pair_specs(height, parts, step)
            out_shape += [jax.ShapeDtypeStruct((height, width), kind)] * 2
        else:
            out_specs.append(
                pl.BlockSpec((height, step), lambda group, at, core: (0, group * 2 * parts + at))
            )
            out_shape.append(jax.ShapeDtypeStruct((height, 2 * width), kind))

    def kernel(core_ref, rows_ref, *refs):
        block_ref = refs[-1]
        load_block(refs[:8], block_ref)
        total = matmul(rows_ref[...], block_ref[...])
        side = pl.program_id(1) % 2
        place = 8
        values = []
        for extra in extras:
            if isinstance(extra, tuple):
                values.append(jnp.where(side == 0, refs[place][...], refs[place + 1][...]))
                place += 2
            else:
                values.append(refs[place][...])
                place += 1
        for (_, _, paired), result in zip(out_types, finish(total, *values)):
            if paired:
                for index in (0, 1):

                    @pl.when(side == index)
                    def _():
                        refs[place + index][...] = result

                place += 2
            else:
                refs[place][...] = result
                place += 1

    return call_kernel(
        kernel,
        core,
        24,
        (2, 2 * parts),
        in_specs,
        out_specs,
        out_shape,
        operands,
        [pltpu.VMEM((rows.shape[1], step), jnp.bfloat16)],
    )


def contract_rows(core, pair, weight, start, width, parts):
    step = width // (2 * parts)
    height = pair[0].shape[0]
    shape = (height, 4 * weight[0].shape[0])

    def kernel(core_ref, own_ref, send_ref, *refs):
        out_ref, block_ref = refs[-2:]

        @pl.when((pl.program_id(0) == 0) & (pl.program_id(1) == 0))
        def _():
            out_ref[...] = jnp.zeros_like(out_ref)

        load_block(refs[:8], block_ref)
        rows = jnp.where(pl.program_id(1) % 2 == 0, own_ref[...], send_ref[...])
        out_ref[...] += outer_cols(rows, block_ref[...])

    return call_kernel(
        kernel,
        core,
        20,
        (2, 2 * parts),
        pair_specs(height, parts, step) + weight_specs(weight, start, parts, step),
        pl.BlockSpec(shape, lambda group, at, core: (0, 0)),
        jax.ShapeDtypeStruct(shape, jnp.float32),
        (*pair, *weight),
        [pltpu.VMEM((shape[1], step), jnp.bfloat16)],
    )


def grad_parts(terms):
    depth = terms[0][0].shape[1]
    half, quarter, eighth = depth // 2, depth // 4, depth // 8
    widths = [units.shape[1] // 2 for _, _, units, _ in terms]
    total_width = sum(widths)

    def kernel(*refs):
        y_keep, y_send, x_keep, x_send = refs[-4:]
        start = 0
        for index, width in enumerate(widths):
            rows, rows_other, units, units_other = refs[4 * index :][:4]
            columns = slice(start, start + width)
            start += width
            for core in (0, 1):
                here = slice(core * half, (core + 1) * half)
                there = slice((1 - core) * half, (2 - core) * half)
                total = inner_rows(rows[:, here], units[...])
                total = total + inner_rows(rows_other[:, there], units_other[...])
                total = total.astype(jnp.bfloat16)
                place = slice(core * quarter, (core + 1) * quarter)

                @pl.when(pl.program_id(0) == 0)
                def _():
                    y_keep[place, columns] = total[:quarter]

                @pl.when(pl.program_id(0) == 1)
                def _():
                    y_send[place, columns] = total[:quarter]

                place = slice(core * eighth, (core + 1) * eighth)
                x_keep[place, columns] = total[quarter : quarter + eighth]
                x_send[place, columns] = total[quarter + eighth :]

    in_specs = []
    for (rows, _, units, _), width in zip(terms, widths):
        whole = pl.BlockSpec(rows.shape, lambda group: (0, 0))
        own = pl.BlockSpec((units.shape[0], width), lambda group: (0, group))
        in_specs += [whole, whole, own, own]
    y_spec = pl.BlockSpec((half, total_width), lambda group: (0, 0))
    x_spec = pl.BlockSpec((quarter, total_width), lambda group: (group, 0))
    return pl.pallas_call(
        kernel,
        grid=(2,),
        in_specs=in_specs,
        out_specs=[y_spec, y_spec, x_spec, x_spec],
        out_shape=[jax.ShapeDtypeStruct((half, total_width), jnp.bfloat16)] * 4,
        **kernel_options(24),
    )(*[array for term in terms for array in term])


def gelu_pair(inputs):
    share = 0.5 * (1.0 + lax.erf(inputs * 0.5**0.5))
    slope = share + inputs * (jnp.exp(-0.5 * inputs * inputs) * (0.5 / jnp.pi) ** 0.5)
    return (inputs * share).astype(jnp.bfloat16), slope.astype(jnp.bfloat16)


def data_plan(
    tokens,
    segments,
    w_qkv,
    bias_qv,
    w_out,
    bias_out,
    ln1_gain,
    ln1_bias,
    w_up,
    bias_up,
    w_down,
    bias_down,
    ln2_gain,
    ln2_bias,
    d_out,
):
    low, wide = jnp.bfloat16, jnp.float32
    dp_index = lax.axis_index("dp")
    tensor_index = lax.axis_index("tensor")
    width = tokens.shape[1]
    head_width = w_qkv.shape[2]
    unit_width = w_up.shape[1]
    groups = (0, 1)

    place = jnp.arange(width)
    block = ((place // 32) % 4) * 4 + ((place // 128) % 2) * 2 + place // 512
    source = (dp_index ^ block) * 64 + ((place // 256) % 2) * 32 + place % 32
    order = (jnp.arange(width)[:, None] == source[None, :]).astype(low)

    def group_of(vector, group, size):
        return lax.dynamic_slice_in_dim(vector, (tensor_index ^ group) * size, size, axis=-1)

    def whole_of(parts):
        left, right = parts
        return jnp.where(
            tensor_index == 0,
            jnp.concatenate([left, right], axis=-1),
            jnp.concatenate([right, left], axis=-1),
        )

    vectors = jnp.dot(
        jnp.stack([bias_out, ln1_gain, ln1_bias, bias_down, ln2_gain, ln2_bias]),
        order.astype(wide),
        precision=lax.Precision.HIGHEST,
    )
    bias_out, ln1_gain, ln1_bias, bias_down, ln2_gain, ln2_bias = [vectors[i] for i in range(6)]
    own_rows = matmul(tokens, order).astype(low)
    cotangent = matmul(d_out, order)

    which = lax.dynamic_slice_in_dim(segments, tensor_index, 1, axis=0)
    column, row = which.reshape(SEQ, 1), which

    rows = tokens.shape[0]
    blank = jnp.zeros((head_width,), wide)
    qkv_bias = jnp.concatenate(
        [
            vector
            for group in groups
            for vector in (
                group_of(bias_qv[0], group, head_width),
                blank,
                group_of(bias_qv[1], group, head_width),
            )
        ]
    )[None]
    units_bias = jnp.concatenate([group_of(bias_up, group, unit_width) for group in groups])[None]

    core_index = dp_index % 2
    core = core_index.astype(jnp.int32).reshape(1)

    def ordered(own, send):
        return jnp.where(
            core_index == 0,
            jnp.concatenate([own, send], axis=-1),
            jnp.concatenate([send, own], axis=-1),
        )

    def attention_work(weight):
        (qkv,) = expand_rows(
            jnp.zeros_like(core),
            own_rows,
            weight,
            0,
            3 * head_width,
            1,
            lambda total, bias: ((total + bias).astype(low),),
            [qkv_bias],
            [(rows, low, False)],
        )
        context, logsum = attend_rows_forward(core, qkv, column, row)
        return dict(qkv=qkv, context=context, logsum=logsum)

    def units_work(weight, results):
        attn_rows = contract_rows(core, results["context"], weight, unit_width, head_width, 1)
        z_one = own_rows.astype(wide) + attn_rows + bias_out
        h_one, scaled_one, spread_one = norm_forward(z_one, ln1_gain, ln1_bias)
        h_low = h_one.astype(low)
        act_own, act_send, slope_own, slope_send = expand_rows(
            core,
            h_low,
            weight,
            0,
            unit_width,
            1,
            lambda total, bias: gelu_pair(total + bias),
            [units_bias],
            [(rows, low, True), (rows, low, True)],
        )
        return results | dict(
            norm=(h_one, scaled_one, spread_one),
            h_low=h_low,
            activation=(act_own, act_send),
            slope=(slope_own, slope_send),
        )

    (qkv_w, up_out_w, down_w), made = gather_weights(
        [
            jnp.concatenate([w_qkv[0], w_qkv[1], w_qkv[2]], axis=1),
            jnp.concatenate([w_up, w_out.T], axis=1),
            w_down.T,
        ],
        attention_work,
        units_work,
    )
    qkv, context, logsum = made["qkv"], made["context"], made["logsum"]
    h_one, scaled_one, spread_one = made["norm"]
    h_low, activation, slope = made["h_low"], made["activation"], made["slope"]
    mlp_rows = contract_rows(core, activation, down_w, 0, unit_width, 1)
    z_two = h_one + mlp_rows + bias_down
    normed, scaled_two, spread_two = norm_forward(z_two, ln2_gain, ln2_bias)
    output_low = normed.astype(low)

    grad_two, d_gain_two, d_offset_two = norm_backward(cotangent, scaled_two, spread_two, ln2_gain)
    d_bias_down = jnp.sum(grad_two, axis=0)
    grad_two_low = grad_two.astype(low)

    after = lax.optimization_barrier
    grad_two_low, slope, activation = after((grad_two_low, slope, activation))
    grad_two_other, act_other = over_core(grad_two_low), over_core(activation[1])

    def finish_units(total, slope):
        units = (total * slope.astype(wide)).astype(low)
        return units, jnp.sum(units.astype(wide), axis=0, keepdims=True)

    *d_up, d_bias_units = expand_rows(
        core,
        grad_two_low,
        down_w,
        0,
        unit_width,
        1,
        finish_units,
        [slope],
        [(rows, low, True), (1, wide, False)],
    )
    (grad_two_other, act_other, d_up, h_low, own_rows, context) = after(
        (grad_two_other, act_other, d_up, h_low, own_rows, context)
    )
    up_other, h_other = over_core(d_up[1]), over_core(h_low)
    rows_other, context_other = over_core(own_rows), over_core(context[1])
    down_sum = grad_parts([(grad_two_low, grad_two_other, activation[0], act_other)])
    down_sum, up_other, h_other, rows_other, context_other, d_up = after(
        (down_sum, up_other, h_other, rows_other, context_other, d_up)
    )
    down_sum = scatter_first(down_sum)
    mlp_back = contract_rows(core, d_up, up_out_w, 0, unit_width, 1)
    grad_one, d_gain_one, d_offset_one = norm_backward(
        mlp_back + grad_two, scaled_one, spread_one, ln1_gain
    )
    d_bias_out = jnp.sum(grad_one, axis=0)
    grad_one_low = grad_one.astype(low)
    up_sum = grad_parts([(h_low, h_other, d_up[0], up_other)])
    (d_ctx,) = expand_rows(
        core,
        grad_one_low,
        up_out_w,
        unit_width,
        head_width,
        1,
        lambda total: (total.astype(low),),
        [],
        [(rows, low, False)],
    )
    down_sum, up_sum, d_ctx, grad_one_low = after((down_sum, up_sum, d_ctx, grad_one_low))
    down_sum, up_sum = scatter_both(down_sum, up_sum)
    grad_one_other = over_core(grad_one_low)
    d_qkv, qkv_sums = attend_rows_backward(core, qkv, column, row, logsum, d_ctx)
    qkv_other = over_core(d_qkv[1])
    last_sum = grad_parts(
        [
            (own_rows, rows_other, d_qkv[0], qkv_other),
            (grad_one_low, grad_one_other, context[0], context_other),
        ]
    )
    down_sum, up_sum, last_sum, d_qkv = after((down_sum, up_sum, last_sum, d_qkv))
    up_sum, last_sum = scatter_both(up_sum, last_sum)
    down_sum = scatter_near(down_sum)
    narrow = jnp.dot(
        jnp.stack([d_bias_out, d_gain_one, d_offset_one, d_bias_down, d_gain_two, d_offset_two]),
        order.astype(wide).T,
        precision=lax.Precision.HIGHEST,
    )
    size = head_width // 2

    def qkv_row(part):
        return whole_of(
            [
                ordered(*[total[:, (3 * group + part) * size :][:, :size] for total in qkv_sums])
                for group in groups
            ]
        )

    def unit_rows():
        half = unit_width // 2
        pieces = [
            [d_bias_units[:, (2 * group + side) * half :][:, :half] for side in (0, 1)] for group in groups
        ]
        pieces = [
            [jnp.where(core_index == 0, own, send), jnp.where(core_index == 0, send, own)]
            for own, send in pieces
        ]
        first, last = [jnp.concatenate(piece) for piece in pieces]
        return [jnp.where(tensor_index == 0, first, last), jnp.where(tensor_index == 0, last, first)]

    small = jnp.concatenate([narrow, qkv_row(0), qkv_row(2), *unit_rows()])
    down_sum, up_sum, last_sum, d_qkv, output_low = after((down_sum, up_sum, last_sum, d_qkv, output_low))
    up_sum = scatter_near(up_sum)
    last_sum = scatter_second(last_sum)
    attn_back = contract_rows(core, d_qkv, qkv_w, 0, 3 * head_width, 3)
    grad_rows = attn_back + grad_one
    upper = grad_rows.astype(low)
    lower = (grad_rows - upper.astype(wide)).astype(low)
    grad_tokens = outer_cols(upper, order) + outer_cols(lower, order)
    output = outer_cols(output_low, order).astype(low)
    up_sum, last_sum, small, down_sum = after((up_sum, last_sum, small, down_sum))
    last_sum = scatter_near(last_sum)
    small = sum_chips(small)
    pairs = scatter_last([down_sum, up_sum], core_index)
    last_sum, small, pairs = after((last_sum, small, pairs))
    small = sum_near(small)
    pairs = pairs + scatter_last([last_sum], core_index)
    grad_w_down = jnp.concatenate(pairs[0], axis=1).T
    grad_w_up = jnp.concatenate(pairs[1], axis=1)
    size = head_width // 2
    parts = [
        jnp.concatenate([part[:, at * size :][:, :size] for part in pairs[2]], axis=1) for at in range(4)
    ]
    grad_w_qkv = jnp.stack(parts[:3])
    grad_w_out = parts[3].T

    return (
        output,
        grad_tokens,
        grad_w_qkv,
        small[6:8],
        grad_w_out,
        small[0],
        small[1],
        small[2],
        grad_w_up,
        small[8:].reshape(-1),
        grad_w_down,
        small[3],
        small[4],
        small[5],
    )


def local(*arrays):
    tokens = arrays[0]
    sizes = (lax.axis_size("dp"), lax.axis_size("tensor"))
    if sizes == (16, 2) and tokens.shape == (SEQ, 1024):
        return data_plan(*arrays)
    return tensor_plan(*arrays)


def solution(mesh):
    return jax.shard_map(
        local,
        mesh=mesh,
        in_specs=(
            P(("dp", "tensor"), None),
            P("dp", None),
            P(None, "dp", "tensor"),
            P(),
            P("tensor", "dp"),
            P(),
            P(),
            P(),
            P("dp", "tensor"),
            P(),
            P("tensor", "dp"),
            P(),
            P(),
            P(),
            P(("dp", "tensor"), None),
        ),
        out_specs=(
            P(("dp", "tensor"), None),
            P(("dp", "tensor"), None),
            P(None, "dp", "tensor"),
            P(),
            P("tensor", "dp"),
            P(),
            P(),
            P(),
            P("dp", "tensor"),
            P(),
            P("tensor", "dp"),
            P(),
            P(),
            P(),
        ),
        check_vma=False,
    )
```

```python
import functools

import jax
import jax.numpy as jnp
from jax import lax
from jax.experimental import pallas as pl
from jax.experimental.pallas import tpu as pltpu
from jax.sharding import PartitionSpec as P

HEAD_DIM = 64
SEQ = 512


eps = 1e-12


def matmul(left, right):
    return jnp.dot(left, right, preferred_element_type=jnp.float32)


def inner_rows(left, right):
    return lax.dot_general(
        left, right, (((0,), (0,)), ((), ())), preferred_element_type=jnp.float32
    )


def outer_cols(left, right):
    return lax.dot_general(
        left, right, (((1,), (1,)), ((), ())), preferred_element_type=jnp.float32
    )


def norm_forward(inputs, gain_vec, offset):
    center = jnp.mean(inputs, axis=-1, keepdims=True)
    spread = lax.rsqrt(jnp.mean(jnp.square(inputs - center), axis=-1, keepdims=True) + eps)
    scaled = (inputs - center) * spread
    return (scaled * gain_vec + offset, scaled, spread)


def norm_backward(gradient, scaled, spread, gain_vec):
    d_gain = jnp.sum(gradient * scaled, axis=0)
    d_offset = jnp.sum(gradient, axis=0)
    d_scaled = gradient * gain_vec
    d_inputs = spread * (
        d_scaled
        - jnp.mean(d_scaled, axis=-1, keepdims=True)
        - scaled * jnp.mean(d_scaled * scaled, axis=-1, keepdims=True)
    )
    return (d_inputs, d_gain, d_offset)


def masked_scores(queries, key_rows, segment):
    raw_scores = jnp.einsum("qhd,khd->hqk", queries, key_rows, preferred_element_type=jnp.float32)
    same_doc = segment[:, None] == segment[None, :]
    return jnp.where(same_doc[None], raw_scores * HEAD_DIM ** (-0.5), -1000000000.0)


def attend_forward(block):
    queries, key_rows, value_rows, segment = block
    scores = masked_scores(queries, key_rows, segment)
    row_max = jnp.max(scores, axis=-1, keepdims=True)
    exponent = jnp.exp(scores - row_max)
    row_total = jnp.sum(exponent, axis=-1, keepdims=True)
    probabilities = (exponent / row_total).astype(jnp.bfloat16)
    context = jnp.einsum(
        "hqk,khd->qhd", probabilities, value_rows, preferred_element_type=jnp.float32
    )
    return (context.astype(jnp.bfloat16), row_max[..., 0] + jnp.log(row_total[..., 0]))


def attend_backward(block):
    queries, key_rows, value_rows, segment, logsum, d_context = block
    scores = masked_scores(queries, key_rows, segment)
    probabilities = jnp.exp(scores - logsum[..., None])
    d_probs = jnp.einsum("qhd,khd->hqk", d_context, value_rows, preferred_element_type=jnp.float32)
    row_dot = jnp.sum(d_probs * probabilities, axis=-1, keepdims=True)
    d_raw = (probabilities * (d_probs - row_dot) * HEAD_DIM ** (-0.5)).astype(jnp.bfloat16)
    d_queries = jnp.einsum("hqk,khd->qhd", d_raw, key_rows, preferred_element_type=jnp.float32)
    d_keys = jnp.einsum("hqk,qhd->khd", d_raw, queries, preferred_element_type=jnp.float32)
    d_values = jnp.einsum(
        "hqk,qhd->khd",
        probabilities.astype(jnp.bfloat16),
        d_context,
        preferred_element_type=jnp.float32,
    )
    return (
        d_queries.astype(jnp.bfloat16),
        d_keys.astype(jnp.bfloat16),
        d_values.astype(jnp.bfloat16),
    )


def tensor_plan(
    tokens,
    segments,
    w_qkv,
    bias_qv,
    w_out,
    bias_out,
    ln1_gain,
    ln1_bias,
    w_up,
    bias_up,
    w_down,
    bias_down,
    ln2_gain,
    ln2_bias,
    d_out,
):
    qkv_w, out_w, up_w, down_w = (
        lax.all_gather(w_qkv, "dp", axis=1, tiled=True),
        lax.all_gather(w_out, "dp", axis=1, tiled=True),
        lax.all_gather(w_up, "dp", axis=0, tiled=True),
        lax.all_gather(w_down, "dp", axis=1, tiled=True),
    )
    head_width = qkv_w.shape[2]
    unit_width = up_w.shape[1]
    tensor_index = lax.axis_index("tensor")
    bias_query = lax.dynamic_slice_in_dim(bias_qv[0], tensor_index * head_width, head_width)
    bias_value = lax.dynamic_slice_in_dim(bias_qv[1], tensor_index * head_width, head_width)
    bias_units = lax.dynamic_slice_in_dim(bias_up, tensor_index * unit_width, unit_width)
    block_rows = lax.all_gather(tokens, "tensor", axis=0, tiled=True)
    pieces = [
        matmul(block_rows, qkv_w[0]) + bias_query,
        matmul(block_rows, qkv_w[1]),
        matmul(block_rows, qkv_w[2]) + bias_value,
    ]
    qkv_all = jnp.concatenate(pieces, axis=1)
    qkv_rows = qkv_all.astype(jnp.bfloat16)
    group_rows = qkv_rows.shape[0]
    shape_seq = (segments.shape[0], SEQ, head_width // HEAD_DIM, HEAD_DIM)
    queries = qkv_rows[:, :head_width].reshape(shape_seq)
    key_rows = qkv_rows[:, head_width : 2 * head_width].reshape(shape_seq)
    value_rows = qkv_rows[:, 2 * head_width :].reshape(shape_seq)
    context, logsum = lax.map(attend_forward, (queries, key_rows, value_rows, segments))
    context_rows = context.reshape(group_rows, head_width)
    attn_rows = lax.psum_scatter(
        matmul(context_rows, out_w).astype(jnp.bfloat16), "tensor", scatter_dimension=0, tiled=True
    ).astype(jnp.float32)
    z_one = tokens.astype(jnp.float32) + attn_rows + bias_out
    h_one, scaled_one, spread_one = norm_forward(z_one, ln1_gain, ln1_bias)
    h_low = h_one.astype(jnp.bfloat16)
    pieces = [matmul(lax.all_gather(h_low, "tensor", axis=0, tiled=True), up_w) + bias_units]
    up_all = pieces[0]
    activation = jax.nn.gelu(up_all, approximate=False).astype(jnp.bfloat16)
    mlp_rows = lax.psum_scatter(
        matmul(activation, down_w).astype(jnp.bfloat16), "tensor", scatter_dimension=0, tiled=True
    ).astype(jnp.float32)
    z_two = h_one + mlp_rows + bias_down
    normed, scaled_two, spread_two = norm_forward(z_two, ln2_gain, ln2_bias)
    output = normed.astype(jnp.bfloat16)
    qkv_w, out_w, up_w, down_w = (
        lax.all_gather(w_qkv, "dp", axis=1, tiled=True),
        lax.all_gather(w_out, "dp", axis=1, tiled=True),
        lax.all_gather(w_up, "dp", axis=0, tiled=True),
        lax.all_gather(w_down, "dp", axis=1, tiled=True),
    )
    grad_two, d_gain_two, d_offset_two = norm_backward(
        d_out.astype(jnp.float32), scaled_two, spread_two, ln2_gain
    )
    d_bias_down = jnp.sum(grad_two, axis=0)
    grad_two_low = grad_two.astype(jnp.bfloat16)
    block_rows = lax.all_gather(grad_two_low, "tensor", axis=0, tiled=True)
    d_act = outer_cols(block_rows, down_w)
    d_wdown, d_act = (inner_rows(activation, block_rows), d_act)
    gelu_pull = jax.vjp(lambda inputs: jax.nn.gelu(inputs, approximate=False), up_all)[1]
    d_up = gelu_pull(d_act)[0].astype(jnp.bfloat16)
    d_bias_units = jnp.sum(d_up, axis=0, dtype=jnp.float32)
    d_bias_up = lax.dynamic_update_slice_in_dim(
        jnp.zeros(bias_up.shape, jnp.float32), d_bias_units, tensor_index * unit_width, 0
    )
    mlp_back = lax.psum_scatter(
        outer_cols(d_up, up_w).astype(jnp.bfloat16), "tensor", scatter_dimension=0, tiled=True
    ).astype(jnp.float32)
    d_wup = inner_rows(lax.all_gather(h_low, "tensor", axis=0, tiled=True), d_up)
    grad_one, d_gain_one, d_offset_one = norm_backward(
        mlp_back + grad_two, scaled_one, spread_one, ln1_gain
    )
    d_bias_out = jnp.sum(grad_one, axis=0)
    grad_one_low = grad_one.astype(jnp.bfloat16)
    block_rows = lax.all_gather(grad_one_low, "tensor", axis=0, tiled=True)
    d_ctx = outer_cols(block_rows, out_w)
    d_wout, d_ctx = (inner_rows(context_rows, block_rows), d_ctx)
    d_ctx_low = d_ctx.astype(jnp.bfloat16).reshape(shape_seq)
    d_queries, d_keys, d_values = lax.map(
        attend_backward, (queries, key_rows, value_rows, segments, logsum, d_ctx_low)
    )
    d_qkv = jnp.concatenate(
        [
            d_queries.reshape(group_rows, head_width),
            d_keys.reshape(group_rows, head_width),
            d_values.reshape(group_rows, head_width),
        ],
        axis=1,
    )
    bias_pair = jnp.stack(
        [
            jnp.sum(d_qkv[:, :head_width], axis=0, dtype=jnp.float32),
            jnp.sum(d_qkv[:, 2 * head_width :], axis=0, dtype=jnp.float32),
        ]
    )
    d_bias_qv = lax.dynamic_update_slice_in_dim(
        jnp.zeros(bias_qv.shape, jnp.float32), bias_pair, tensor_index * head_width, 1
    )
    total_rows = outer_cols(d_qkv[:, :head_width], qkv_w[0])
    total_rows = total_rows + outer_cols(d_qkv[:, head_width : 2 * head_width], qkv_w[1])
    attn_back = lax.psum_scatter(
        (total_rows + outer_cols(d_qkv[:, 2 * head_width :], qkv_w[2])).astype(jnp.bfloat16),
        "tensor",
        scatter_dimension=0,
        tiled=True,
    ).astype(jnp.float32)
    grad_tokens = attn_back + grad_one
    block_rows = lax.all_gather(tokens, "tensor", axis=0, tiled=True)
    grads_part = d_qkv
    grads_part = grads_part.reshape(block_rows.shape[0], 3, head_width)
    d_wqkv = jnp.einsum("rd,rtc->tdc", block_rows, grads_part, preferred_element_type=jnp.float32)
    grad_w_qkv, grad_w_out, grad_w_up, grad_w_down = (
        lax.psum_scatter(d_wqkv.astype(jnp.bfloat16), "dp", scatter_dimension=1, tiled=True).astype(
            jnp.float32
        ),
        lax.psum_scatter(d_wout.astype(jnp.bfloat16), "dp", scatter_dimension=1, tiled=True).astype(
            jnp.float32
        ),
        lax.psum_scatter(d_wup.astype(jnp.bfloat16), "dp", scatter_dimension=0, tiled=True).astype(
            jnp.float32
        ),
        lax.psum_scatter(
            d_wdown.astype(jnp.bfloat16), "dp", scatter_dimension=1, tiled=True
        ).astype(jnp.float32),
    )
    small_grads = lax.psum(
        (
            d_bias_qv,
            d_bias_out,
            d_gain_one,
            d_offset_one,
            d_bias_up,
            d_bias_down,
            d_gain_two,
            d_offset_two,
        ),
        ("dp", "tensor"),
    )
    return (
        output,
        grad_tokens,
        grad_w_qkv,
        small_grads[0],
        grad_w_out,
        small_grads[1],
        small_grads[2],
        small_grads[3],
        grad_w_up,
        small_grads[4],
        grad_w_down,
        small_grads[5],
        small_grads[6],
        small_grads[7],
    )


def swap(array, name, mask):
    size = lax.axis_size(name)
    return lax.ppermute(array, name, [(index, index ^ mask) for index in range(size)])


def over_y(array):
    return swap(array, "tensor", 1)


def over_x(array):
    return swap(array, "dp", 2)


def over_core(array):
    return swap(array, "dp", 1)


def over_z(array, step):
    return swap(array, "dp", 4 * step)


def gather_first(stack):
    rows = stack[0].shape[0] // 2
    left, right = [jnp.concatenate([part[half * rows :][:rows] for part in stack]) for half in (0, 1)]
    return left, over_x(left), right, over_y(right)


def gather_second(parts):
    left = jnp.concatenate(parts[:2])
    right = jnp.concatenate(parts[2:])
    return left, over_y(left), right, over_x(right), over_core(left), over_core(right)


def gather_last(parts):
    left, left_other, right, right_other, left_core, right_core = parts
    here = (left, left_other, right, right_other)
    return here + (left_core, over_core(left_other), right_core, over_core(right_other))


def gather_weights(shards, first_work, second_work):
    after = lax.optimization_barrier
    one, two, three = shards
    one = [one] + [over_z(one, step) for step in (1, 2, 3)]
    two = [two, over_z(two, 1)]
    one, two, three = after((one, two, three))
    one = gather_first(one)
    two = two + [over_z(two[0], 2)]
    three = [three, over_z(three, 1)]
    one, two, three = after((one, two, three))
    one = gather_second(one)
    two = two + [over_z(two[1], 2)]
    one, two, three = after((one, two, three))
    two = gather_first(two)
    one = gather_last(one)
    three = three + [over_z(three[0], 2)]
    one, two, three = after((one, two, three))
    two = gather_second(two)
    three = three + [over_z(three[1], 2)]
    made = first_work(one)
    two, three, made = after((two, three, made))
    three = gather_first(three)
    two = gather_last(two)
    two, three, made = after((two, three, made))
    three = gather_second(three)
    made = second_work(two, made)
    three, made = after((three, made))
    return (one, two, gather_last(three)), made


def add_low(left, right):
    return (left.astype(jnp.float32) + right.astype(jnp.float32)).astype(jnp.bfloat16)


def beside(left, right):
    return jnp.concatenate([left, right])


def scatter_first(parts):
    y_keep, y_send, x_keep, x_send = parts
    return scatter_first_sum(y_keep, over_y(y_send), x_keep, over_x(x_send))


def scatter_first_sum(y_keep, y_other, x_keep, x_other):
    rows = y_keep.shape[0] // 4
    left, left_send = [
        beside(*[add_low(y_keep[at:][:rows], y_other[at:][:rows]) for at in (start, start + 2 * rows)])
        for start in (0, rows)
    ]
    return (
        left,
        left_send,
        add_low(x_keep[: 2 * rows], x_other[: 2 * rows]),
        add_low(x_keep[2 * rows :], x_other[2 * rows :]),
    )


def scatter_second(parts):
    left, left_send, right, right_send = parts
    return add_low(left, over_x(left_send)), add_low(right, over_y(right_send))


def scatter_both(later, sooner):
    left, left_send, right, right_send = later
    y_keep, y_send, x_keep, x_send = sooner
    rows = left.shape[0]
    x_other = over_x(beside(left_send, x_send))
    y_other = over_y(beside(right_send, y_send))
    done = add_low(left, x_other[:rows]), add_low(right, y_other[:rows])
    return done, scatter_first_sum(y_keep, y_other[rows:], x_keep, x_other[rows:])


def scatter_near(parts):
    quarters = [part.reshape(2, 4, part.shape[0] // 8, -1) for part in parts]
    stack = [
        jnp.concatenate([half[core, step] for half in quarters for core in (0, 1)]) for step in range(4)
    ]
    terms = [stack[0]] + [over_z(stack[step], step) for step in (1, 2, 3)]
    terms = [term.astype(jnp.float32) for term in terms]
    return (terms[0] + terms[1]) + (terms[2] + terms[3])


def scatter_last(sums, core_index):
    rows = sums[0].shape[0] // 4
    split = [
        [jnp.concatenate([total[at:][:rows] for at in (core * rows, (core + 2) * rows)]) for core in (0, 1)]
        for total in sums
    ]
    other = over_core(jnp.concatenate([send for _, send in split], axis=1))
    width = sums[0].shape[1]
    pairs = []
    for index, (keep, _) in enumerate(split):
        there = other[:, index * width :][:, :width]
        pairs.append((jnp.where(core_index == 0, keep, there), jnp.where(core_index == 0, there, keep)))
    return pairs


def sum_chips(array):
    array = array + over_core(array)
    array = array + over_x(array)
    return array + over_y(array)


def sum_near(array):
    array = array + over_z(array, 1)
    return array + over_z(array, 2)


def head_scores(queries, key_rows, same_doc):
    raw_scores = outer_cols(queries * jnp.bfloat16(HEAD_DIM ** (-0.5)), key_rows)
    return jnp.where(same_doc, raw_scores, -1000000000.0)


def attend_forward_kernel(
    core_ref, q_ref, k_ref, v_ref, column_ref, row_ref, own_ref, send_ref, logsum_ref
):
    lane = lax.broadcasted_iota(jnp.int32, q_ref.shape, 1) // HEAD_DIM
    same_doc = column_ref[...] == row_ref[...]
    value_rows = v_ref[...]
    contexts = []
    logsums = []
    for head in (0, 1):
        queries = jnp.where(lane == head, q_ref[...], jnp.bfloat16(0))
        scores = head_scores(queries, k_ref[...], same_doc)
        row_max = jnp.max(scores, axis=-1, keepdims=True)
        exponent = jnp.exp(scores - row_max)
        row_total = jnp.sum(exponent, axis=-1, keepdims=True)
        probabilities = (exponent * (1.0 / row_total)).astype(jnp.bfloat16)
        contexts.append(matmul(probabilities, value_rows))
        logsums.append(row_max + jnp.log(row_total))
    context = jnp.where(lane == 0, contexts[0], contexts[1]).astype(jnp.bfloat16)
    own = pl.program_id(1) < pl.num_programs(1) // 2

    @pl.when(own)
    def _():
        own_ref[...] = context

    @pl.when(jnp.logical_not(own))
    def _():
        send_ref[...] = context

    logsum_ref[...] = jnp.where(lane == 0, logsums[0], logsums[1])


def attend_backward_kernel(
    core_ref,
    q_ref,
    k_ref,
    v_ref,
    column_ref,
    row_ref,
    logsum_ref,
    dctx_ref,
    own_ref,
    send_ref,
    own_sum_ref,
    send_sum_ref,
):
    lane = lax.broadcasted_iota(jnp.int32, q_ref.shape, 1) // HEAD_DIM
    same_doc = column_ref[...] == row_ref[...]
    key_rows = k_ref[...]
    value_rows = v_ref[...]
    results = []
    for head in (0, 1):
        queries = jnp.where(lane == head, q_ref[...], jnp.bfloat16(0))
        d_context = jnp.where(lane == head, dctx_ref[...], jnp.bfloat16(0))
        scores = head_scores(queries, key_rows, same_doc)
        place = head * HEAD_DIM
        probabilities = jnp.exp(scores - logsum_ref[:, place : place + 1])
        d_probs = outer_cols(d_context, value_rows)
        row_dot = jnp.sum(d_probs * probabilities, axis=-1, keepdims=True)
        d_raw = (probabilities * (d_probs - row_dot) * HEAD_DIM ** (-0.5)).astype(jnp.bfloat16)
        results.append(
            (
                matmul(d_raw, key_rows),
                inner_rows(d_raw, queries),
                inner_rows(probabilities.astype(jnp.bfloat16), d_context),
            )
        )
    half = pl.num_programs(1) // 2
    at = pl.program_id(1)
    own = at < half
    first = pl.program_id(0) * 3 * half + jnp.where(own, at, at - half)
    for part, (left, right) in enumerate(zip(*results)):
        place = pl.ds(pl.multiple_of((first + part * half) * 128, 128), 128)
        gradient = jnp.where(lane == 0, left, right).astype(jnp.bfloat16)

        total = jnp.sum(gradient.astype(jnp.float32), axis=0, keepdims=True)

        @pl.when(own)
        def _():
            own_ref[:, place] = gradient
            own_sum_ref[:, place] = total

        @pl.when(jnp.logical_not(own))
        def _():
            send_ref[:, place] = gradient
            send_sum_ref[:, place] = total


def kernel_options(mebibytes):
    return dict(
        cost_estimate=pl.CostEstimate(flops=0, bytes_accessed=0, transcendentals=0),
        compiler_params=pltpu.CompilerParams(vmem_limit_bytes=mebibytes << 20),
    )


def call_kernel(
    kernel, core, mebibytes, grid, in_specs, out_specs, out_shape, operands, scratch_shapes=()
):
    return pl.pallas_call(
        kernel,
        grid_spec=pltpu.PrefetchScalarGridSpec(
            num_scalar_prefetch=1,
            grid=grid,
            in_specs=in_specs,
            out_specs=out_specs,
            scratch_shapes=scratch_shapes,
        ),
        out_shape=out_shape,
        **kernel_options(mebibytes),
    )(core, *operands)


def attention_inputs(rows, pairs, column, row):
    def place(part):
        return lambda group, at, core: (
            0,
            group * 3 * pairs + part * pairs + (at ^ (core[0] * (pairs // 2))),
        )

    whole = lambda group, at, core: (0, 0)
    return [pl.BlockSpec((rows, 128), place(part)) for part in range(3)] + [
        pl.BlockSpec(column.shape, whole),
        pl.BlockSpec(row.shape, whole),
    ]


def attend_rows_forward(core, qkv, column, row):
    rows, pairs = qkv.shape[0], qkv.shape[1] // 768
    half = pairs // 2
    own = pl.BlockSpec((rows, 128), lambda group, at, core: (0, group * half + jnp.minimum(at, half - 1)))
    send = pl.BlockSpec((rows, 128), lambda group, at, core: (0, group * half + jnp.maximum(at - half, 0)))
    flat = pl.BlockSpec((rows, 128), lambda group, at, core: (0, group * pairs + at))
    pair_shape = jax.ShapeDtypeStruct((rows, pairs * 128), jnp.bfloat16)
    own, send, logsum = call_kernel(
        attend_forward_kernel,
        core,
        16,
        (2, pairs),
        attention_inputs(rows, pairs, column, row),
        [own, send, flat],
        [pair_shape, pair_shape, jax.ShapeDtypeStruct((rows, pairs * 256), jnp.float32)],
        (qkv, qkv, qkv, column, row),
    )
    return (own, send), logsum


def attend_rows_backward(core, qkv, column, row, logsum, d_context):
    rows, pairs = qkv.shape[0], qkv.shape[1] // 768
    flat = pl.BlockSpec((rows, 128), lambda group, at, core: (0, group * pairs + at))
    pair_spec = pl.BlockSpec((rows, qkv.shape[1] // 2), lambda group, at, core: (0, 0))
    pair_shape = jax.ShapeDtypeStruct((rows, qkv.shape[1] // 2), jnp.bfloat16)
    sum_spec = pl.BlockSpec((1, qkv.shape[1] // 2), lambda group, at, core: (0, 0))
    sum_shape = jax.ShapeDtypeStruct((1, qkv.shape[1] // 2), jnp.float32)
    own, send, own_sum, send_sum = call_kernel(
        attend_backward_kernel,
        core,
        20,
        (2, pairs),
        attention_inputs(rows, pairs, column, row) + [flat, flat],
        [pair_spec, pair_spec, sum_spec, sum_spec],
        [pair_shape, pair_shape, sum_shape, sum_shape],
        (qkv, qkv, qkv, column, row, logsum, d_context),
    )
    return (own, send), (own_sum, send_sum)


def weight_specs(weight, start, parts, step):
    rows = weight[0].shape[0]
    first, last = start // step, 2 * parts - 1

    def column(at, core):
        return first + (at ^ core[0])

    left = pl.BlockSpec(
        (rows, step), lambda group, at, core: (0, column(jnp.where(group == 0, at, last), core))
    )
    other = pl.BlockSpec(
        (rows, step), lambda group, at, core: (0, column(jnp.where(group == 1, at, 0), core))
    )
    right = pl.BlockSpec((rows // 2, step), lambda group, at, core: (group, column(at, core)))
    return [left, other, right, right] * 2


def load_block(refs, block_ref):
    for group in (0, 1):

        @pl.when(pl.program_id(0) == group)
        def _():
            start = 0
            for part in (refs[group], refs[2], refs[3], refs[4 + group], refs[6], refs[7]):
                block_ref[start : start + part.shape[0], :] = part[...]
                start += part.shape[0]


def pair_specs(height, parts, step):
    return [pl.BlockSpec((height, step), lambda group, at, core: (0, group * parts + at // 2))] * 2


def expand_rows(core, rows, weight, start, width, parts, finish, extras, out_types):
    step = width // (2 * parts)
    in_specs = [pl.BlockSpec(rows.shape, lambda group, at, core: (0, 0))]
    in_specs += weight_specs(weight, start, parts, step)
    operands = [rows, *weight]
    for extra in extras:
        if isinstance(extra, tuple):
            in_specs += pair_specs(extra[0].shape[0], parts, step)
            operands += extra
        else:
            in_specs.append(
                pl.BlockSpec((1, step), lambda group, at, core: (0, group * 2 * parts + (at ^ core[0])))
            )
            operands.append(extra)
    out_specs, out_shape = [], []
    for height, kind, paired in out_types:
        if paired:
            out_specs += pair_specs(height, parts, step)
            out_shape += [jax.ShapeDtypeStruct((height, width), kind)] * 2
        else:
            out_specs.append(
                pl.BlockSpec((height, step), lambda group, at, core: (0, group * 2 * parts + at))
            )
            out_shape.append(jax.ShapeDtypeStruct((height, 2 * width), kind))

    def kernel(core_ref, rows_ref, *refs):
        block_ref = refs[-1]
        load_block(refs[:8], block_ref)
        total = matmul(rows_ref[...], block_ref[...])
        side = pl.program_id(1) % 2
        place = 8
        values = []
        for extra in extras:
            if isinstance(extra, tuple):
                values.append(jnp.where(side == 0, refs[place][...], refs[place + 1][...]))
                place += 2
            else:
                values.append(refs[place][...])
                place += 1
        for (_, _, paired), result in zip(out_types, finish(total, *values)):
            if paired:
                for index in (0, 1):

                    @pl.when(side == index)
                    def _():
                        refs[place + index][...] = result

                place += 2
            else:
                refs[place][...] = result
                place += 1

    return call_kernel(
        kernel,
        core,
        24,
        (2, 2 * parts),
        in_specs,
        out_specs,
        out_shape,
        operands,
        [pltpu.VMEM((rows.shape[1], step), jnp.bfloat16)],
    )


def contract_rows(core, pair, weight, start, width, parts):
    step = width // (2 * parts)
    height = pair[0].shape[0]
    shape = (height, 4 * weight[0].shape[0])

    def kernel(core_ref, own_ref, send_ref, *refs):
        out_ref, block_ref = refs[-2:]

        @pl.when((pl.program_id(0) == 0) & (pl.program_id(1) == 0))
        def _():
            out_ref[...] = jnp.zeros_like(out_ref)

        load_block(refs[:8], block_ref)
        rows = jnp.where(pl.program_id(1) % 2 == 0, own_ref[...], send_ref[...])
        out_ref[...] += outer_cols(rows, block_ref[...])

    return call_kernel(
        kernel,
        core,
        20,
        (2, 2 * parts),
        pair_specs(height, parts, step) + weight_specs(weight, start, parts, step),
        pl.BlockSpec(shape, lambda group, at, core: (0, 0)),
        jax.ShapeDtypeStruct(shape, jnp.float32),
        (*pair, *weight),
        [pltpu.VMEM((shape[1], step), jnp.bfloat16)],
    )


def grad_parts(terms):
    depth = terms[0][0].shape[1]
    half, quarter, eighth = depth // 2, depth // 4, depth // 8
    widths = [units.shape[1] // 2 for _, _, units, _ in terms]
    total_width = sum(widths)

    def kernel(*refs):
        y_keep, y_send, x_keep, x_send = refs[-4:]
        start = 0
        for index, width in enumerate(widths):
            rows, rows_other, units, units_other = refs[4 * index :][:4]
            columns = slice(start, start + width)
            start += width
            for core in (0, 1):
                here = slice(core * half, (core + 1) * half)
                there = slice((1 - core) * half, (2 - core) * half)
                total = inner_rows(rows[:, here], units[...])
                total = total + inner_rows(rows_other[:, there], units_other[...])
                total = total.astype(jnp.bfloat16)
                place = slice(core * quarter, (core + 1) * quarter)

                @pl.when(pl.program_id(0) == 0)
                def _():
                    y_keep[place, columns] = total[:quarter]

                @pl.when(pl.program_id(0) == 1)
                def _():
                    y_send[place, columns] = total[:quarter]

                place = slice(core * eighth, (core + 1) * eighth)
                x_keep[place, columns] = total[quarter : quarter + eighth]
                x_send[place, columns] = total[quarter + eighth :]

    in_specs = []
    for (rows, _, units, _), width in zip(terms, widths):
        whole = pl.BlockSpec(rows.shape, lambda group: (0, 0))
        own = pl.BlockSpec((units.shape[0], width), lambda group: (0, group))
        in_specs += [whole, whole, own, own]
    y_spec = pl.BlockSpec((half, total_width), lambda group: (0, 0))
    x_spec = pl.BlockSpec((quarter, total_width), lambda group: (group, 0))
    return pl.pallas_call(
        kernel,
        grid=(2,),
        in_specs=in_specs,
        out_specs=[y_spec, y_spec, x_spec, x_spec],
        out_shape=[jax.ShapeDtypeStruct((half, total_width), jnp.bfloat16)] * 4,
        **kernel_options(24),
    )(*[array for term in terms for array in term])


def gelu_pair(inputs):
    share = 0.5 * (1.0 + lax.erf(inputs * 0.5**0.5))
    slope = share + inputs * (jnp.exp(-0.5 * inputs * inputs) * (0.5 / jnp.pi) ** 0.5)
    return (inputs * share).astype(jnp.bfloat16), slope.astype(jnp.bfloat16)


def data_plan(
    tokens,
    segments,
    w_qkv,
    bias_qv,
    w_out,
    bias_out,
    ln1_gain,
    ln1_bias,
    w_up,
    bias_up,
    w_down,
    bias_down,
    ln2_gain,
    ln2_bias,
    d_out,
):
    low, wide = jnp.bfloat16, jnp.float32
    dp_index = lax.axis_index("dp")
    tensor_index = lax.axis_index("tensor")
    width = tokens.shape[1]
    head_width = w_qkv.shape[2]
    unit_width = w_up.shape[1]
    groups = (0, 1)

    place = jnp.arange(width)
    block = ((place // 32) % 4) * 4 + ((place // 128) % 2) * 2 + place // 512
    source = (dp_index ^ block) * 64 + ((place // 256) % 2) * 32 + place % 32
    order = (jnp.arange(width)[:, None] == source[None, :]).astype(low)

    def group_of(vector, group, size):
        return lax.dynamic_slice_in_dim(vector, (tensor_index ^ group) * size, size, axis=-1)

    def whole_of(parts):
        left, right = parts
        return jnp.where(
            tensor_index == 0,
            jnp.concatenate([left, right], axis=-1),
            jnp.concatenate([right, left], axis=-1),
        )

    vectors = jnp.dot(
        jnp.stack([bias_out, ln1_gain, ln1_bias, bias_down, ln2_gain, ln2_bias]),
        order.astype(wide),
        precision=lax.Precision.HIGHEST,
    )
    bias_out, ln1_gain, ln1_bias, bias_down, ln2_gain, ln2_bias = [vectors[i] for i in range(6)]
    own_rows = matmul(tokens, order).astype(low)
    cotangent = matmul(d_out, order)

    which = lax.dynamic_slice_in_dim(segments, tensor_index, 1, axis=0)
    column, row = which.reshape(SEQ, 1), which

    rows = tokens.shape[0]
    blank = jnp.zeros((head_width,), wide)
    qkv_bias = jnp.concatenate(
        [
            vector
            for group in groups
            for vector in (
                group_of(bias_qv[0], group, head_width),
                blank,
                group_of(bias_qv[1], group, head_width),
            )
        ]
    )[None]
    units_bias = jnp.concatenate([group_of(bias_up, group, unit_width) for group in groups])[None]

    core_index = dp_index % 2
    core = core_index.astype(jnp.int32).reshape(1)

    def ordered(own, send):
        return jnp.where(
            core_index == 0,
            jnp.concatenate([own, send], axis=-1),
            jnp.concatenate([send, own], axis=-1),
        )

    def attention_work(weight):
        (qkv,) = expand_rows(
            jnp.zeros_like(core),
            own_rows,
            weight,
            0,
            3 * head_width,
            1,
            lambda total, bias: ((total + bias).astype(low),),
            [qkv_bias],
            [(rows, low, False)],
        )
        context, logsum = attend_rows_forward(core, qkv, column, row)
        return dict(qkv=qkv, context=context, logsum=logsum)

    def units_work(weight, results):
        attn_rows = contract_rows(core, results["context"], weight, unit_width, head_width, 1)
        z_one = own_rows.astype(wide) + attn_rows + bias_out
        h_one, scaled_one, spread_one = norm_forward(z_one, ln1_gain, ln1_bias)
        h_low = h_one.astype(low)
        act_own, act_send, slope_own, slope_send = expand_rows(
            core,
            h_low,
            weight,
            0,
            unit_width,
            1,
            lambda total, bias: gelu_pair(total + bias),
            [units_bias],
            [(rows, low, True), (rows, low, True)],
        )
        return results | dict(
            norm=(h_one, scaled_one, spread_one),
            h_low=h_low,
            activation=(act_own, act_send),
            slope=(slope_own, slope_send),
        )

    (qkv_w, up_out_w, down_w), made = gather_weights(
        [
            jnp.concatenate([w_qkv[0], w_qkv[1], w_qkv[2]], axis=1),
            jnp.concatenate([w_up, w_out.T], axis=1),
            w_down.T,
        ],
        attention_work,
        units_work,
    )
    qkv, context, logsum = made["qkv"], made["context"], made["logsum"]
    h_one, scaled_one, spread_one = made["norm"]
    h_low, activation, slope = made["h_low"], made["activation"], made["slope"]
    mlp_rows = contract_rows(core, activation, down_w, 0, unit_width, 1)
    z_two = h_one + mlp_rows + bias_down
    normed, scaled_two, spread_two = norm_forward(z_two, ln2_gain, ln2_bias)
    output_low = normed.astype(low)

    grad_two, d_gain_two, d_offset_two = norm_backward(cotangent, scaled_two, spread_two, ln2_gain)
    d_bias_down = jnp.sum(grad_two, axis=0)
    grad_two_low = grad_two.astype(low)

    after = lax.optimization_barrier
    grad_two_low, slope, activation = after((grad_two_low, slope, activation))
    grad_two_other, act_other = over_core(grad_two_low), over_core(activation[1])

    def finish_units(total, slope):
        units = (total * slope.astype(wide)).astype(low)
        return units, jnp.sum(units.astype(wide), axis=0, keepdims=True)

    *d_up, d_bias_units = expand_rows(
        core,
        grad_two_low,
        down_w,
        0,
        unit_width,
        1,
        finish_units,
        [slope],
        [(rows, low, True), (1, wide, False)],
    )
    (grad_two_other, act_other, d_up, h_low, own_rows, context) = after(
        (grad_two_other, act_other, d_up, h_low, own_rows, context)
    )
    up_other, h_other = over_core(d_up[1]), over_core(h_low)
    rows_other, context_other = over_core(own_rows), over_core(context[1])
    down_sum = grad_parts([(grad_two_low, grad_two_other, activation[0], act_other)])
    down_sum, up_other, h_other, rows_other, context_other, d_up = after(
        (down_sum, up_other, h_other, rows_other, context_other, d_up)
    )
    down_sum = scatter_first(down_sum)
    mlp_back = contract_rows(core, d_up, up_out_w, 0, unit_width, 1)
    grad_one, d_gain_one, d_offset_one = norm_backward(
        mlp_back + grad_two, scaled_one, spread_one, ln1_gain
    )
    grad_one_low = grad_one.astype(low)
    up_sum = grad_parts([(h_low, h_other, d_up[0], up_other)])
    (d_ctx,) = expand_rows(
        core,
        grad_one_low,
        up_out_w,
        unit_width,
        head_width,
        1,
        lambda total: (total.astype(low),),
        [],
        [(rows, low, False)],
    )
    down_sum, up_sum, d_ctx, grad_one_low = after((down_sum, up_sum, d_ctx, grad_one_low))
    down_sum, up_sum = scatter_both(down_sum, up_sum)
    grad_one_other = over_core(grad_one_low)
    d_qkv, qkv_sums = attend_rows_backward(core, qkv, column, row, logsum, d_ctx)
    qkv_other = over_core(d_qkv[1])
    last_sum = grad_parts(
        [
            (own_rows, rows_other, d_qkv[0], qkv_other),
            (grad_one_low, grad_one_other, context[0], context_other),
        ]
    )
    down_sum, up_sum, last_sum, d_qkv, grad_one, d_gain_one = after(
        (down_sum, up_sum, last_sum, d_qkv, grad_one, d_gain_one)
    )
    d_bias_out = jnp.sum(grad_one, axis=0)
    up_sum, last_sum = scatter_both(up_sum, last_sum)
    down_sum = scatter_near(down_sum)
    narrow = jnp.dot(
        jnp.stack([d_bias_out, d_gain_one, d_offset_one, d_bias_down, d_gain_two, d_offset_two]),
        order.astype(wide).T,
        precision=lax.Precision.HIGHEST,
    )
    size = head_width // 2

    def qkv_row(part):
        return whole_of(
            [
                ordered(*[total[:, (3 * group + part) * size :][:, :size] for total in qkv_sums])
                for group in groups
            ]
        )

    def unit_rows():
        half = unit_width // 2
        pieces = [
            [d_bias_units[:, (2 * group + side) * half :][:, :half] for side in (0, 1)] for group in groups
        ]
        pieces = [
            [jnp.where(core_index == 0, own, send), jnp.where(core_index == 0, send, own)]
            for own, send in pieces
        ]
        first, last = [jnp.concatenate(piece) for piece in pieces]
        return [jnp.where(tensor_index == 0, first, last), jnp.where(tensor_index == 0, last, first)]

    small = jnp.concatenate([narrow, qkv_row(0), qkv_row(2), *unit_rows()])
    down_sum, up_sum, last_sum, d_qkv, output_low = after((down_sum, up_sum, last_sum, d_qkv, output_low))
    up_sum = scatter_near(up_sum)
    last_sum = scatter_second(last_sum)
    attn_back = contract_rows(core, d_qkv, qkv_w, 0, 3 * head_width, 3)
    grad_rows = attn_back + grad_one
    upper = grad_rows.astype(low)
    lower = (grad_rows - upper.astype(wide)).astype(low)
    grad_tokens = outer_cols(upper, order) + outer_cols(lower, order)
    output = outer_cols(output_low, order).astype(low)
    up_sum, last_sum, small, down_sum = after((up_sum, last_sum, small, down_sum))
    last_sum = scatter_near(last_sum)
    small = sum_near(sum_chips(small))
    pairs = scatter_last([down_sum, up_sum], core_index)
    grad_w_down = jnp.concatenate(pairs[0], axis=1).T
    grad_w_up = jnp.concatenate(pairs[1], axis=1)
    last_sum, small, grad_w_down, grad_w_up = after((last_sum, small, grad_w_down, grad_w_up))
    last_pair = scatter_last([last_sum], core_index)[0]
    size = head_width // 2
    parts = [
        jnp.concatenate([part[:, at * size :][:, :size] for part in last_pair], axis=1) for at in range(4)
    ]
    grad_w_qkv = jnp.stack(parts[:3])
    grad_w_out = parts[3].T

    return (
        output,
        grad_tokens,
        grad_w_qkv,
        small[6:8],
        grad_w_out,
        small[0],
        small[1],
        small[2],
        grad_w_up,
        small[8:].reshape(-1),
        grad_w_down,
        small[3],
        small[4],
        small[5],
    )


def local(*arrays):
    tokens = arrays[0]
    sizes = (lax.axis_size("dp"), lax.axis_size("tensor"))
    if sizes == (16, 2) and tokens.shape == (SEQ, 1024):
        return data_plan(*arrays)
    return tensor_plan(*arrays)


def solution(mesh):
    return jax.shard_map(
        local,
        mesh=mesh,
        in_specs=(
            P(("dp", "tensor"), None),
            P("dp", None),
            P(None, "dp", "tensor"),
            P(),
            P("tensor", "dp"),
            P(),
            P(),
            P(),
            P("dp", "tensor"),
            P(),
            P("tensor", "dp"),
            P(),
            P(),
            P(),
            P(("dp", "tensor"), None),
        ),
        out_specs=(
            P(("dp", "tensor"), None),
            P(("dp", "tensor"), None),
            P(None, "dp", "tensor"),
            P(),
            P("tensor", "dp"),
            P(),
            P(),
            P(),
            P("dp", "tensor"),
            P(),
            P("tensor", "dp"),
            P(),
            P(),
            P(),
        ),
        check_vma=False,
    )
```

```python
import functools

import jax
import jax.numpy as jnp
from jax import lax
from jax.experimental import pallas as pl
from jax.experimental.pallas import tpu as pltpu
from jax.sharding import PartitionSpec as P

HEAD_DIM = 64
SEQ = 512


eps = 1e-12


def matmul(left, right):
    return jnp.dot(left, right, preferred_element_type=jnp.float32)


def inner_rows(left, right):
    return lax.dot_general(
        left, right, (((0,), (0,)), ((), ())), preferred_element_type=jnp.float32
    )


def outer_cols(left, right):
    return lax.dot_general(
        left, right, (((1,), (1,)), ((), ())), preferred_element_type=jnp.float32
    )


def norm_forward(inputs, gain_vec, offset):
    center = jnp.mean(inputs, axis=-1, keepdims=True)
    spread = lax.rsqrt(jnp.mean(jnp.square(inputs - center), axis=-1, keepdims=True) + eps)
    scaled = (inputs - center) * spread
    return (scaled * gain_vec + offset, scaled, spread)


def norm_backward(gradient, scaled, spread, gain_vec):
    d_gain = jnp.sum(gradient * scaled, axis=0)
    d_offset = jnp.sum(gradient, axis=0)
    d_scaled = gradient * gain_vec
    d_inputs = spread * (
        d_scaled
        - jnp.mean(d_scaled, axis=-1, keepdims=True)
        - scaled * jnp.mean(d_scaled * scaled, axis=-1, keepdims=True)
    )
    return (d_inputs, d_gain, d_offset)


def masked_scores(queries, key_rows, segment):
    raw_scores = jnp.einsum("qhd,khd->hqk", queries, key_rows, preferred_element_type=jnp.float32)
    same_doc = segment[:, None] == segment[None, :]
    return jnp.where(same_doc[None], raw_scores * HEAD_DIM ** (-0.5), -1000000000.0)


def attend_forward(block):
    queries, key_rows, value_rows, segment = block
    scores = masked_scores(queries, key_rows, segment)
    row_max = jnp.max(scores, axis=-1, keepdims=True)
    exponent = jnp.exp(scores - row_max)
    row_total = jnp.sum(exponent, axis=-1, keepdims=True)
    probabilities = (exponent / row_total).astype(jnp.bfloat16)
    context = jnp.einsum(
        "hqk,khd->qhd", probabilities, value_rows, preferred_element_type=jnp.float32
    )
    return (context.astype(jnp.bfloat16), row_max[..., 0] + jnp.log(row_total[..., 0]))


def attend_backward(block):
    queries, key_rows, value_rows, segment, logsum, d_context = block
    scores = masked_scores(queries, key_rows, segment)
    probabilities = jnp.exp(scores - logsum[..., None])
    d_probs = jnp.einsum("qhd,khd->hqk", d_context, value_rows, preferred_element_type=jnp.float32)
    row_dot = jnp.sum(d_probs * probabilities, axis=-1, keepdims=True)
    d_raw = (probabilities * (d_probs - row_dot) * HEAD_DIM ** (-0.5)).astype(jnp.bfloat16)
    d_queries = jnp.einsum("hqk,khd->qhd", d_raw, key_rows, preferred_element_type=jnp.float32)
    d_keys = jnp.einsum("hqk,qhd->khd", d_raw, queries, preferred_element_type=jnp.float32)
    d_values = jnp.einsum(
        "hqk,qhd->khd",
        probabilities.astype(jnp.bfloat16),
        d_context,
        preferred_element_type=jnp.float32,
    )
    return (
        d_queries.astype(jnp.bfloat16),
        d_keys.astype(jnp.bfloat16),
        d_values.astype(jnp.bfloat16),
    )


def tensor_plan(
    tokens,
    segments,
    w_qkv,
    bias_qv,
    w_out,
    bias_out,
    ln1_gain,
    ln1_bias,
    w_up,
    bias_up,
    w_down,
    bias_down,
    ln2_gain,
    ln2_bias,
    d_out,
):
    qkv_w, out_w, up_w, down_w = (
        lax.all_gather(w_qkv, "dp", axis=1, tiled=True),
        lax.all_gather(w_out, "dp", axis=1, tiled=True),
        lax.all_gather(w_up, "dp", axis=0, tiled=True),
        lax.all_gather(w_down, "dp", axis=1, tiled=True),
    )
    head_width = qkv_w.shape[2]
    unit_width = up_w.shape[1]
    tensor_index = lax.axis_index("tensor")
    bias_query = lax.dynamic_slice_in_dim(bias_qv[0], tensor_index * head_width, head_width)
    bias_value = lax.dynamic_slice_in_dim(bias_qv[1], tensor_index * head_width, head_width)
    bias_units = lax.dynamic_slice_in_dim(bias_up, tensor_index * unit_width, unit_width)
    block_rows = lax.all_gather(tokens, "tensor", axis=0, tiled=True)
    pieces = [
        matmul(block_rows, qkv_w[0]) + bias_query,
        matmul(block_rows, qkv_w[1]),
        matmul(block_rows, qkv_w[2]) + bias_value,
    ]
    qkv_all = jnp.concatenate(pieces, axis=1)
    qkv_rows = qkv_all.astype(jnp.bfloat16)
    group_rows = qkv_rows.shape[0]
    shape_seq = (segments.shape[0], SEQ, head_width // HEAD_DIM, HEAD_DIM)
    queries = qkv_rows[:, :head_width].reshape(shape_seq)
    key_rows = qkv_rows[:, head_width : 2 * head_width].reshape(shape_seq)
    value_rows = qkv_rows[:, 2 * head_width :].reshape(shape_seq)
    context, logsum = lax.map(attend_forward, (queries, key_rows, value_rows, segments))
    context_rows = context.reshape(group_rows, head_width)
    attn_rows = lax.psum_scatter(
        matmul(context_rows, out_w).astype(jnp.bfloat16), "tensor", scatter_dimension=0, tiled=True
    ).astype(jnp.float32)
    z_one = tokens.astype(jnp.float32) + attn_rows + bias_out
    h_one, scaled_one, spread_one = norm_forward(z_one, ln1_gain, ln1_bias)
    h_low = h_one.astype(jnp.bfloat16)
    pieces = [matmul(lax.all_gather(h_low, "tensor", axis=0, tiled=True), up_w) + bias_units]
    up_all = pieces[0]
    activation = jax.nn.gelu(up_all, approximate=False).astype(jnp.bfloat16)
    mlp_rows = lax.psum_scatter(
        matmul(activation, down_w).astype(jnp.bfloat16), "tensor", scatter_dimension=0, tiled=True
    ).astype(jnp.float32)
    z_two = h_one + mlp_rows + bias_down
    normed, scaled_two, spread_two = norm_forward(z_two, ln2_gain, ln2_bias)
    output = normed.astype(jnp.bfloat16)
    qkv_w, out_w, up_w, down_w = (
        lax.all_gather(w_qkv, "dp", axis=1, tiled=True),
        lax.all_gather(w_out, "dp", axis=1, tiled=True),
        lax.all_gather(w_up, "dp", axis=0, tiled=True),
        lax.all_gather(w_down, "dp", axis=1, tiled=True),
    )
    grad_two, d_gain_two, d_offset_two = norm_backward(
        d_out.astype(jnp.float32), scaled_two, spread_two, ln2_gain
    )
    d_bias_down = jnp.sum(grad_two, axis=0)
    grad_two_low = grad_two.astype(jnp.bfloat16)
    block_rows = lax.all_gather(grad_two_low, "tensor", axis=0, tiled=True)
    d_act = outer_cols(block_rows, down_w)
    d_wdown, d_act = (inner_rows(activation, block_rows), d_act)
    gelu_pull = jax.vjp(lambda inputs: jax.nn.gelu(inputs, approximate=False), up_all)[1]
    d_up = gelu_pull(d_act)[0].astype(jnp.bfloat16)
    d_bias_units = jnp.sum(d_up, axis=0, dtype=jnp.float32)
    d_bias_up = lax.dynamic_update_slice_in_dim(
        jnp.zeros(bias_up.shape, jnp.float32), d_bias_units, tensor_index * unit_width, 0
    )
    mlp_back = lax.psum_scatter(
        outer_cols(d_up, up_w).astype(jnp.bfloat16), "tensor", scatter_dimension=0, tiled=True
    ).astype(jnp.float32)
    d_wup = inner_rows(lax.all_gather(h_low, "tensor", axis=0, tiled=True), d_up)
    grad_one, d_gain_one, d_offset_one = norm_backward(
        mlp_back + grad_two, scaled_one, spread_one, ln1_gain
    )
    d_bias_out = jnp.sum(grad_one, axis=0)
    grad_one_low = grad_one.astype(jnp.bfloat16)
    block_rows = lax.all_gather(grad_one_low, "tensor", axis=0, tiled=True)
    d_ctx = outer_cols(block_rows, out_w)
    d_wout, d_ctx = (inner_rows(context_rows, block_rows), d_ctx)
    d_ctx_low = d_ctx.astype(jnp.bfloat16).reshape(shape_seq)
    d_queries, d_keys, d_values = lax.map(
        attend_backward, (queries, key_rows, value_rows, segments, logsum, d_ctx_low)
    )
    d_qkv = jnp.concatenate(
        [
            d_queries.reshape(group_rows, head_width),
            d_keys.reshape(group_rows, head_width),
            d_values.reshape(group_rows, head_width),
        ],
        axis=1,
    )
    bias_pair = jnp.stack(
        [
            jnp.sum(d_qkv[:, :head_width], axis=0, dtype=jnp.float32),
            jnp.sum(d_qkv[:, 2 * head_width :], axis=0, dtype=jnp.float32),
        ]
    )
    d_bias_qv = lax.dynamic_update_slice_in_dim(
        jnp.zeros(bias_qv.shape, jnp.float32), bias_pair, tensor_index * head_width, 1
    )
    total_rows = outer_cols(d_qkv[:, :head_width], qkv_w[0])
    total_rows = total_rows + outer_cols(d_qkv[:, head_width : 2 * head_width], qkv_w[1])
    attn_back = lax.psum_scatter(
        (total_rows + outer_cols(d_qkv[:, 2 * head_width :], qkv_w[2])).astype(jnp.bfloat16),
        "tensor",
        scatter_dimension=0,
        tiled=True,
    ).astype(jnp.float32)
    grad_tokens = attn_back + grad_one
    block_rows = lax.all_gather(tokens, "tensor", axis=0, tiled=True)
    grads_part = d_qkv
    grads_part = grads_part.reshape(block_rows.shape[0], 3, head_width)
    d_wqkv = jnp.einsum("rd,rtc->tdc", block_rows, grads_part, preferred_element_type=jnp.float32)
    grad_w_qkv, grad_w_out, grad_w_up, grad_w_down = (
        lax.psum_scatter(d_wqkv.astype(jnp.bfloat16), "dp", scatter_dimension=1, tiled=True).astype(
            jnp.float32
        ),
        lax.psum_scatter(d_wout.astype(jnp.bfloat16), "dp", scatter_dimension=1, tiled=True).astype(
            jnp.float32
        ),
        lax.psum_scatter(d_wup.astype(jnp.bfloat16), "dp", scatter_dimension=0, tiled=True).astype(
            jnp.float32
        ),
        lax.psum_scatter(
            d_wdown.astype(jnp.bfloat16), "dp", scatter_dimension=1, tiled=True
        ).astype(jnp.float32),
    )
    small_grads = lax.psum(
        (
            d_bias_qv,
            d_bias_out,
            d_gain_one,
            d_offset_one,
            d_bias_up,
            d_bias_down,
            d_gain_two,
            d_offset_two,
        ),
        ("dp", "tensor"),
    )
    return (
        output,
        grad_tokens,
        grad_w_qkv,
        small_grads[0],
        grad_w_out,
        small_grads[1],
        small_grads[2],
        small_grads[3],
        grad_w_up,
        small_grads[4],
        grad_w_down,
        small_grads[5],
        small_grads[6],
        small_grads[7],
    )


def swap(array, name, mask):
    size = lax.axis_size(name)
    return lax.ppermute(array, name, [(index, index ^ mask) for index in range(size)])


def over_y(array):
    return swap(array, "tensor", 1)


def over_x(array):
    return swap(array, "dp", 2)


def over_core(array):
    return swap(array, "dp", 1)


def over_z(array, step):
    return swap(array, "dp", 4 * step)


def gather_first(stack):
    rows = stack[0].shape[0] // 2
    left, right = [jnp.concatenate([part[half * rows :][:rows] for part in stack]) for half in (0, 1)]
    return left, over_x(left), right, over_y(right)


def gather_second(parts):
    left = jnp.concatenate(parts[:2])
    right = jnp.concatenate(parts[2:])
    return left, over_y(left), right, over_x(right), over_core(left), over_core(right)


def gather_last(parts):
    left, left_other, right, right_other, left_core, right_core = parts
    here = (left, left_other, right, right_other)
    return here + (left_core, over_core(left_other), right_core, over_core(right_other))


def gather_weights(shards, first_work, second_work):
    after = lax.optimization_barrier
    one, two, three = shards
    one = [one] + [over_z(one, step) for step in (1, 2, 3)]
    two = [two, over_z(two, 1)]
    one, two, three = after((one, two, three))
    one = gather_first(one)
    two = two + [over_z(two[0], 2)]
    three = [three, over_z(three, 1)]
    one, two, three = after((one, two, three))
    one = gather_second(one)
    two = two + [over_z(two[1], 2)]
    one, two, three = after((one, two, three))
    two = gather_first(two)
    one = gather_last(one)
    three = three + [over_z(three[0], 2)]
    one, two, three = after((one, two, three))
    two = gather_second(two)
    three = three + [over_z(three[1], 2)]
    made = first_work(one)
    two, three, made = after((two, three, made))
    three = gather_first(three)
    two = gather_last(two)
    two, three, made = after((two, three, made))
    three = gather_second(three)
    made = second_work(two, made)
    three, made = after((three, made))
    return (one, two, gather_last(three)), made


def add_low(left, right):
    return (left.astype(jnp.float32) + right.astype(jnp.float32)).astype(jnp.bfloat16)


def beside(left, right):
    return jnp.concatenate([left, right])


def scatter_first(parts):
    y_keep, y_send, x_keep, x_send = parts
    return scatter_first_sum(y_keep, over_y(y_send), x_keep, over_x(x_send))


def scatter_first_sum(y_keep, y_other, x_keep, x_other):
    rows = y_keep.shape[0] // 4
    left, left_send = [
        beside(*[add_low(y_keep[at:][:rows], y_other[at:][:rows]) for at in (start, start + 2 * rows)])
        for start in (0, rows)
    ]
    return (
        left,
        left_send,
        add_low(x_keep[: 2 * rows], x_other[: 2 * rows]),
        add_low(x_keep[2 * rows :], x_other[2 * rows :]),
    )


def scatter_second(parts):
    left, left_send, right, right_send = parts
    return add_low(left, over_x(left_send)), add_low(right, over_y(right_send))


def scatter_both(later, sooner):
    left, left_send, right, right_send = later
    y_keep, y_send, x_keep, x_send = sooner
    rows = left.shape[0]
    x_other = over_x(beside(left_send, x_send))
    y_other = over_y(beside(right_send, y_send))
    done = add_low(left, x_other[:rows]), add_low(right, y_other[:rows])
    return done, scatter_first_sum(y_keep, y_other[rows:], x_keep, x_other[rows:])


def scatter_near(parts):
    quarters = [part.reshape(2, 4, part.shape[0] // 8, -1) for part in parts]
    stack = [
        jnp.concatenate([half[core, step] for half in quarters for core in (0, 1)]) for step in range(4)
    ]
    terms = [stack[0]] + [over_z(stack[step], step) for step in (1, 2, 3)]
    terms = [term.astype(jnp.float32) for term in terms]
    return (terms[0] + terms[1]) + (terms[2] + terms[3])


def scatter_last(sums, core_index):
    rows = sums[0].shape[0] // 4
    split = [
        [jnp.concatenate([total[at:][:rows] for at in (core * rows, (core + 2) * rows)]) for core in (0, 1)]
        for total in sums
    ]
    other = over_core(jnp.concatenate([send for _, send in split], axis=1))
    width = sums[0].shape[1]
    pairs = []
    for index, (keep, _) in enumerate(split):
        there = other[:, index * width :][:, :width]
        pairs.append((jnp.where(core_index == 0, keep, there), jnp.where(core_index == 0, there, keep)))
    return pairs


def sum_chips(array):
    array = array + over_core(array)
    array = array + over_x(array)
    return array + over_y(array)


def sum_near(array):
    array = array + over_z(array, 1)
    return array + over_z(array, 2)


def head_scores(queries, key_rows, same_doc):
    raw_scores = outer_cols(queries * jnp.bfloat16(HEAD_DIM ** (-0.5)), key_rows)
    return jnp.where(same_doc, raw_scores, -1000000000.0)


def attend_forward_kernel(
    core_ref, q_ref, k_ref, v_ref, column_ref, row_ref, own_ref, send_ref, prob_ref
):
    lane = lax.broadcasted_iota(jnp.int32, q_ref.shape, 1) // HEAD_DIM
    same_doc = column_ref[...] == row_ref[...]
    value_rows = v_ref[...]
    contexts = []
    for head in (0, 1):
        queries = jnp.where(lane == head, q_ref[...], jnp.bfloat16(0))
        scores = head_scores(queries, k_ref[...], same_doc)
        row_max = jnp.max(scores, axis=-1, keepdims=True)
        exponent = jnp.exp(scores - row_max)
        row_total = jnp.sum(exponent, axis=-1, keepdims=True)
        probabilities = (exponent * (1.0 / row_total)).astype(jnp.bfloat16)
        prob_ref[head] = probabilities
        contexts.append(matmul(probabilities, value_rows))
    context = jnp.where(lane == 0, contexts[0], contexts[1]).astype(jnp.bfloat16)
    own = pl.program_id(1) < pl.num_programs(1) // 2

    @pl.when(own)
    def _():
        own_ref[...] = context

    @pl.when(jnp.logical_not(own))
    def _():
        send_ref[...] = context


def attend_backward_kernel(
    core_ref,
    q_ref,
    k_ref,
    v_ref,
    prob_ref,
    dctx_ref,
    own_ref,
    send_ref,
    own_sum_ref,
    send_sum_ref,
):
    lane = lax.broadcasted_iota(jnp.int32, q_ref.shape, 1) // HEAD_DIM
    scale = HEAD_DIM ** (-0.5)
    key_rows = k_ref[...]
    value_rows = v_ref[...]
    results = []
    for head in (0, 1):
        queries = jnp.where(lane == head, q_ref[...], jnp.bfloat16(0)) * jnp.bfloat16(scale)
        d_context = jnp.where(lane == head, dctx_ref[...], jnp.bfloat16(0))
        probabilities = prob_ref[head].astype(jnp.float32)
        d_probs = outer_cols(d_context, value_rows)
        row_dot = jnp.sum(d_probs * probabilities, axis=-1, keepdims=True)
        d_raw = (probabilities * (d_probs - row_dot)).astype(jnp.bfloat16)
        results.append(
            (
                matmul(d_raw, key_rows) * scale,
                inner_rows(d_raw, queries),
                inner_rows(prob_ref[head], d_context),
            )
        )
    half = pl.num_programs(1) // 2
    at = pl.program_id(1)
    own = at < half
    first = pl.program_id(0) * 3 * half + jnp.where(own, at, at - half)
    for part, (left, right) in enumerate(zip(*results)):
        place = pl.ds(pl.multiple_of((first + part * half) * 128, 128), 128)
        gradient = jnp.where(lane == 0, left, right).astype(jnp.bfloat16)

        total = jnp.sum(gradient.astype(jnp.float32), axis=0, keepdims=True)

        @pl.when(own)
        def _():
            own_ref[:, place] = gradient
            own_sum_ref[:, place] = total

        @pl.when(jnp.logical_not(own))
        def _():
            send_ref[:, place] = gradient
            send_sum_ref[:, place] = total


def kernel_options(mebibytes):
    return dict(
        cost_estimate=pl.CostEstimate(flops=0, bytes_accessed=0, transcendentals=0),
        compiler_params=pltpu.CompilerParams(vmem_limit_bytes=mebibytes << 20),
    )


def call_kernel(
    kernel, core, mebibytes, grid, in_specs, out_specs, out_shape, operands, scratch_shapes=()
):
    return pl.pallas_call(
        kernel,
        grid_spec=pltpu.PrefetchScalarGridSpec(
            num_scalar_prefetch=1,
            grid=grid,
            in_specs=in_specs,
            out_specs=out_specs,
            scratch_shapes=scratch_shapes,
        ),
        out_shape=out_shape,
        **kernel_options(mebibytes),
    )(core, *operands)


def attention_inputs(rows, pairs):
    def place(part):
        return lambda group, at, core: (
            0,
            group * 3 * pairs + part * pairs + (at ^ (core[0] * (pairs // 2))),
        )

    return [pl.BlockSpec((rows, 128), place(part)) for part in range(3)]


def probability_spec(rows, pairs):
    return pl.BlockSpec((2, rows, rows), lambda group, at, core: (group * pairs + at, 0, 0))


def attend_rows_forward(core, qkv, column, row):
    rows, pairs = qkv.shape[0], qkv.shape[1] // 768
    half = pairs // 2
    own = pl.BlockSpec((rows, 128), lambda group, at, core: (0, group * half + jnp.minimum(at, half - 1)))
    send = pl.BlockSpec((rows, 128), lambda group, at, core: (0, group * half + jnp.maximum(at - half, 0)))
    whole = lambda group, at, core: (0, 0)
    pair_shape = jax.ShapeDtypeStruct((rows, pairs * 128), jnp.bfloat16)
    own, send, probabilities = call_kernel(
        attend_forward_kernel,
        core,
        16,
        (2, pairs),
        attention_inputs(rows, pairs)
        + [pl.BlockSpec(column.shape, whole), pl.BlockSpec(row.shape, whole)],
        [own, send, probability_spec(rows, pairs)],
        [pair_shape, pair_shape, jax.ShapeDtypeStruct((4 * pairs, rows, rows), jnp.bfloat16)],
        (qkv, qkv, qkv, column, row),
    )
    return (own, send), probabilities


def attend_rows_backward(core, qkv, probabilities, d_context):
    rows, pairs = qkv.shape[0], qkv.shape[1] // 768
    flat = pl.BlockSpec((rows, 128), lambda group, at, core: (0, group * pairs + at))
    pair_spec = pl.BlockSpec((rows, qkv.shape[1] // 2), lambda group, at, core: (0, 0))
    pair_shape = jax.ShapeDtypeStruct((rows, qkv.shape[1] // 2), jnp.bfloat16)
    sum_spec = pl.BlockSpec((1, qkv.shape[1] // 2), lambda group, at, core: (0, 0))
    sum_shape = jax.ShapeDtypeStruct((1, qkv.shape[1] // 2), jnp.float32)
    own, send, own_sum, send_sum = call_kernel(
        attend_backward_kernel,
        core,
        20,
        (2, pairs),
        attention_inputs(rows, pairs) + [probability_spec(rows, pairs), flat],
        [pair_spec, pair_spec, sum_spec, sum_spec],
        [pair_shape, pair_shape, sum_shape, sum_shape],
        (qkv, qkv, qkv, probabilities, d_context),
    )
    return (own, send), (own_sum, send_sum)


def weight_specs(weight, start, parts, step):
    rows = weight[0].shape[0]
    first, last = start // step, 2 * parts - 1

    def column(at, core):
        return first + (at ^ core[0])

    left = pl.BlockSpec(
        (rows, step), lambda group, at, core: (0, column(jnp.where(group == 0, at, last), core))
    )
    other = pl.BlockSpec(
        (rows, step), lambda group, at, core: (0, column(jnp.where(group == 1, at, 0), core))
    )
    right = pl.BlockSpec((rows // 2, step), lambda group, at, core: (group, column(at, core)))
    return [left, other, right, right] * 2


def load_block(refs, block_ref):
    for group in (0, 1):

        @pl.when(pl.program_id(0) == group)
        def _():
            start = 0
            for part in (refs[group], refs[2], refs[3], refs[4 + group], refs[6], refs[7]):
                block_ref[start : start + part.shape[0], :] = part[...]
                start += part.shape[0]


def pair_specs(height, parts, step):
    return [pl.BlockSpec((height, step), lambda group, at, core: (0, group * parts + at // 2))] * 2


def expand_rows(core, rows, weight, start, width, parts, finish, extras, out_types):
    step = width // (2 * parts)
    in_specs = [pl.BlockSpec(rows.shape, lambda group, at, core: (0, 0))]
    in_specs += weight_specs(weight, start, parts, step)
    operands = [rows, *weight]
    for extra in extras:
        if isinstance(extra, tuple):
            in_specs += pair_specs(extra[0].shape[0], parts, step)
            operands += extra
        else:
            in_specs.append(
                pl.BlockSpec((1, step), lambda group, at, core: (0, group * 2 * parts + (at ^ core[0])))
            )
            operands.append(extra)
    out_specs, out_shape = [], []
    for height, kind, paired in out_types:
        if paired:
            out_specs += pair_specs(height, parts, step)
            out_shape += [jax.ShapeDtypeStruct((height, width), kind)] * 2
        else:
            out_specs.append(
                pl.BlockSpec((height, step), lambda group, at, core: (0, group * 2 * parts + at))
            )
            out_shape.append(jax.ShapeDtypeStruct((height, 2 * width), kind))

    def kernel(core_ref, rows_ref, *refs):
        block_ref = refs[-1]
        load_block(refs[:8], block_ref)
        total = matmul(rows_ref[...], block_ref[...])
        side = pl.program_id(1) % 2
        place = 8
        values = []
        for extra in extras:
            if isinstance(extra, tuple):
                values.append(jnp.where(side == 0, refs[place][...], refs[place + 1][...]))
                place += 2
            else:
                values.append(refs[place][...])
                place += 1
        for (_, _, paired), result in zip(out_types, finish(total, *values)):
            if paired:
                for index in (0, 1):

                    @pl.when(side == index)
                    def _():
                        refs[place + index][...] = result

                place += 2
            else:
                refs[place][...] = result
                place += 1

    return call_kernel(
        kernel,
        core,
        24,
        (2, 2 * parts),
        in_specs,
        out_specs,
        out_shape,
        operands,
        [pltpu.VMEM((rows.shape[1], step), jnp.bfloat16)],
    )


def contract_rows(core, pair, weight, start, width, parts):
    step = width // (2 * parts)
    height = pair[0].shape[0]
    shape = (height, 4 * weight[0].shape[0])

    def kernel(core_ref, own_ref, send_ref, *refs):
        out_ref, block_ref = refs[-2:]

        @pl.when((pl.program_id(0) == 0) & (pl.program_id(1) == 0))
        def _():
            out_ref[...] = jnp.zeros_like(out_ref)

        load_block(refs[:8], block_ref)
        rows = jnp.where(pl.program_id(1) % 2 == 0, own_ref[...], send_ref[...])
        out_ref[...] += outer_cols(rows, block_ref[...])

    return call_kernel(
        kernel,
        core,
        20,
        (2, 2 * parts),
        pair_specs(height, parts, step) + weight_specs(weight, start, parts, step),
        pl.BlockSpec(shape, lambda group, at, core: (0, 0)),
        jax.ShapeDtypeStruct(shape, jnp.float32),
        (*pair, *weight),
        [pltpu.VMEM((shape[1], step), jnp.bfloat16)],
    )


def grad_parts(terms):
    depth = terms[0][0].shape[1]
    half, quarter, eighth = depth // 2, depth // 4, depth // 8
    widths = [units.shape[1] // 2 for _, _, units, _ in terms]
    total_width = sum(widths)

    def kernel(*refs):
        y_keep, y_send, x_keep, x_send = refs[-4:]
        start = 0
        for index, width in enumerate(widths):
            rows, rows_other, units, units_other = refs[4 * index :][:4]
            columns = slice(start, start + width)
            start += width
            for core in (0, 1):
                here = slice(core * half, (core + 1) * half)
                there = slice((1 - core) * half, (2 - core) * half)
                total = inner_rows(rows[:, here], units[...])
                total = total + inner_rows(rows_other[:, there], units_other[...])
                total = total.astype(jnp.bfloat16)
                place = slice(core * quarter, (core + 1) * quarter)

                @pl.when(pl.program_id(0) == 0)
                def _():
                    y_keep[place, columns] = total[:quarter]

                @pl.when(pl.program_id(0) == 1)
                def _():
                    y_send[place, columns] = total[:quarter]

                place = slice(core * eighth, (core + 1) * eighth)
                x_keep[place, columns] = total[quarter : quarter + eighth]
                x_send[place, columns] = total[quarter + eighth :]

    in_specs = []
    for (rows, _, units, _), width in zip(terms, widths):
        whole = pl.BlockSpec(rows.shape, lambda group: (0, 0))
        own = pl.BlockSpec((units.shape[0], width), lambda group: (0, group))
        in_specs += [whole, whole, own, own]
    y_spec = pl.BlockSpec((half, total_width), lambda group: (0, 0))
    x_spec = pl.BlockSpec((quarter, total_width), lambda group: (group, 0))
    return pl.pallas_call(
        kernel,
        grid=(2,),
        in_specs=in_specs,
        out_specs=[y_spec, y_spec, x_spec, x_spec],
        out_shape=[jax.ShapeDtypeStruct((half, total_width), jnp.bfloat16)] * 4,
        **kernel_options(24),
    )(*[array for term in terms for array in term])


def gelu_pair(inputs):
    share = 0.5 * (1.0 + lax.erf(inputs * 0.5**0.5))
    slope = share + inputs * (jnp.exp(-0.5 * inputs * inputs) * (0.5 / jnp.pi) ** 0.5)
    return (inputs * share).astype(jnp.bfloat16), slope.astype(jnp.bfloat16)


def data_plan(
    tokens,
    segments,
    w_qkv,
    bias_qv,
    w_out,
    bias_out,
    ln1_gain,
    ln1_bias,
    w_up,
    bias_up,
    w_down,
    bias_down,
    ln2_gain,
    ln2_bias,
    d_out,
):
    low, wide = jnp.bfloat16, jnp.float32
    dp_index = lax.axis_index("dp")
    tensor_index = lax.axis_index("tensor")
    width = tokens.shape[1]
    head_width = w_qkv.shape[2]
    unit_width = w_up.shape[1]
    groups = (0, 1)

    place = jnp.arange(width)
    block = ((place // 32) % 4) * 4 + ((place // 128) % 2) * 2 + place // 512
    source = (dp_index ^ block) * 64 + ((place // 256) % 2) * 32 + place % 32
    order = (jnp.arange(width)[:, None] == source[None, :]).astype(low)

    def group_of(vector, group, size):
        return lax.dynamic_slice_in_dim(vector, (tensor_index ^ group) * size, size, axis=-1)

    def whole_of(parts):
        left, right = parts
        return jnp.where(
            tensor_index == 0,
            jnp.concatenate([left, right], axis=-1),
            jnp.concatenate([right, left], axis=-1),
        )

    vectors = jnp.dot(
        jnp.stack([bias_out, ln1_gain, ln1_bias, bias_down, ln2_gain, ln2_bias]),
        order.astype(wide),
        precision=lax.Precision.HIGHEST,
    )
    bias_out, ln1_gain, ln1_bias, bias_down, ln2_gain, ln2_bias = [vectors[i] for i in range(6)]
    own_rows = matmul(tokens, order).astype(low)
    cotangent = matmul(d_out, order)

    which = lax.dynamic_slice_in_dim(segments, tensor_index, 1, axis=0)
    column, row = which.reshape(SEQ, 1), which

    rows = tokens.shape[0]
    blank = jnp.zeros((head_width,), wide)
    qkv_bias = jnp.concatenate(
        [
            vector
            for group in groups
            for vector in (
                group_of(bias_qv[0], group, head_width),
                blank,
                group_of(bias_qv[1], group, head_width),
            )
        ]
    )[None]
    units_bias = jnp.concatenate([group_of(bias_up, group, unit_width) for group in groups])[None]

    core_index = dp_index % 2
    core = core_index.astype(jnp.int32).reshape(1)

    def ordered(own, send):
        return jnp.where(
            core_index == 0,
            jnp.concatenate([own, send], axis=-1),
            jnp.concatenate([send, own], axis=-1),
        )

    def attention_work(weight):
        (qkv,) = expand_rows(
            jnp.zeros_like(core),
            own_rows,
            weight,
            0,
            3 * head_width,
            1,
            lambda total, bias: ((total + bias).astype(low),),
            [qkv_bias],
            [(rows, low, False)],
        )
        context, probabilities = attend_rows_forward(core, qkv, column, row)
        return dict(qkv=qkv, context=context, probabilities=probabilities)

    def units_work(weight, results):
        attn_rows = contract_rows(core, results["context"], weight, unit_width, head_width, 1)
        z_one = own_rows.astype(wide) + attn_rows + bias_out
        h_one, scaled_one, spread_one = norm_forward(z_one, ln1_gain, ln1_bias)
        h_low = h_one.astype(low)
        act_own, act_send, slope_own, slope_send = expand_rows(
            core,
            h_low,
            weight,
            0,
            unit_width,
            1,
            lambda total, bias: gelu_pair(total + bias),
            [units_bias],
            [(rows, low, True), (rows, low, True)],
        )
        return results | dict(
            norm=(h_one, scaled_one, spread_one),
            h_low=h_low,
            activation=(act_own, act_send),
            slope=(slope_own, slope_send),
        )

    (qkv_w, up_out_w, down_w), made = gather_weights(
        [
            jnp.concatenate([w_qkv[0], w_qkv[1], w_qkv[2]], axis=1),
            jnp.concatenate([w_up, w_out.T], axis=1),
            w_down.T,
        ],
        attention_work,
        units_work,
    )
    qkv, context, probabilities = made["qkv"], made["context"], made["probabilities"]
    h_one, scaled_one, spread_one = made["norm"]
    h_low, activation, slope = made["h_low"], made["activation"], made["slope"]
    mlp_rows = contract_rows(core, activation, down_w, 0, unit_width, 1)
    z_two = h_one + mlp_rows + bias_down
    normed, scaled_two, spread_two = norm_forward(z_two, ln2_gain, ln2_bias)
    output_low = normed.astype(low)

    grad_two, d_gain_two, d_offset_two = norm_backward(cotangent, scaled_two, spread_two, ln2_gain)
    d_bias_down = jnp.sum(grad_two, axis=0)
    grad_two_low = grad_two.astype(low)

    after = lax.optimization_barrier
    grad_two_low, slope, activation = after((grad_two_low, slope, activation))
    grad_two_other, act_other = over_core(grad_two_low), over_core(activation[1])

    def finish_units(total, slope):
        units = (total * slope.astype(wide)).astype(low)
        return units, jnp.sum(units.astype(wide), axis=0, keepdims=True)

    *d_up, d_bias_units = expand_rows(
        core,
        grad_two_low,
        down_w,
        0,
        unit_width,
        1,
        finish_units,
        [slope],
        [(rows, low, True), (1, wide, False)],
    )
    (grad_two_other, act_other, d_up, h_low, own_rows, context) = after(
        (grad_two_other, act_other, d_up, h_low, own_rows, context)
    )
    up_other, h_other = over_core(d_up[1]), over_core(h_low)
    rows_other, context_other = over_core(own_rows), over_core(context[1])
    down_sum = grad_parts([(grad_two_low, grad_two_other, activation[0], act_other)])
    down_sum, up_other, h_other, rows_other, context_other, d_up = after(
        (down_sum, up_other, h_other, rows_other, context_other, d_up)
    )
    down_sum = scatter_first(down_sum)
    mlp_back = contract_rows(core, d_up, up_out_w, 0, unit_width, 1)
    grad_one, d_gain_one, d_offset_one = norm_backward(
        mlp_back + grad_two, scaled_one, spread_one, ln1_gain
    )
    grad_one_low = grad_one.astype(low)
    up_sum = grad_parts([(h_low, h_other, d_up[0], up_other)])
    (d_ctx,) = expand_rows(
        core,
        grad_one_low,
        up_out_w,
        unit_width,
        head_width,
        1,
        lambda total: (total.astype(low),),
        [],
        [(rows, low, False)],
    )
    down_sum, up_sum, d_ctx, grad_one_low = after((down_sum, up_sum, d_ctx, grad_one_low))
    down_sum, up_sum = scatter_both(down_sum, up_sum)
    grad_one_other = over_core(grad_one_low)
    d_qkv, qkv_sums = attend_rows_backward(core, qkv, probabilities, d_ctx)
    qkv_other = over_core(d_qkv[1])
    last_sum = grad_parts(
        [
            (own_rows, rows_other, d_qkv[0], qkv_other),
            (grad_one_low, grad_one_other, context[0], context_other),
        ]
    )
    down_sum, up_sum, last_sum, d_qkv, grad_one, d_gain_one = after(
        (down_sum, up_sum, last_sum, d_qkv, grad_one, d_gain_one)
    )
    d_bias_out = jnp.sum(grad_one, axis=0)
    up_sum, last_sum = scatter_both(up_sum, last_sum)
    down_sum = scatter_near(down_sum)
    narrow = jnp.dot(
        jnp.stack([d_bias_out, d_gain_one, d_offset_one, d_bias_down, d_gain_two, d_offset_two]),
        order.astype(wide).T,
        precision=lax.Precision.HIGHEST,
    )
    size = head_width // 2

    def qkv_row(part):
        return whole_of(
            [
                ordered(*[total[:, (3 * group + part) * size :][:, :size] for total in qkv_sums])
                for group in groups
            ]
        )

    def unit_rows():
        half = unit_width // 2
        pieces = [
            [d_bias_units[:, (2 * group + side) * half :][:, :half] for side in (0, 1)] for group in groups
        ]
        pieces = [
            [jnp.where(core_index == 0, own, send), jnp.where(core_index == 0, send, own)]
            for own, send in pieces
        ]
        first, last = [jnp.concatenate(piece) for piece in pieces]
        return [jnp.where(tensor_index == 0, first, last), jnp.where(tensor_index == 0, last, first)]

    small = jnp.concatenate([narrow, qkv_row(0), qkv_row(2), *unit_rows()])
    down_sum, up_sum, last_sum, d_qkv, output_low = after((down_sum, up_sum, last_sum, d_qkv, output_low))
    up_sum = scatter_near(up_sum)
    last_sum = scatter_second(last_sum)
    attn_back = contract_rows(core, d_qkv, qkv_w, 0, 3 * head_width, 3)
    grad_rows = attn_back + grad_one
    upper = grad_rows.astype(low)
    lower = (grad_rows - upper.astype(wide)).astype(low)
    grad_tokens = outer_cols(upper, order) + outer_cols(lower, order)
    output = outer_cols(output_low, order).astype(low)
    up_sum, last_sum, small, down_sum = after((up_sum, last_sum, small, down_sum))
    last_sum = scatter_near(last_sum)
    small = sum_near(sum_chips(small))
    pairs = scatter_last([down_sum, up_sum], core_index)
    grad_w_down = jnp.concatenate(pairs[0], axis=1).T
    grad_w_up = jnp.concatenate(pairs[1], axis=1)
    last_sum, small, grad_w_down, grad_w_up = after((last_sum, small, grad_w_down, grad_w_up))
    last_pair = scatter_last([last_sum], core_index)[0]
    size = head_width // 2
    parts = [
        jnp.concatenate([part[:, at * size :][:, :size] for part in last_pair], axis=1) for at in range(4)
    ]
    grad_w_qkv = jnp.stack(parts[:3])
    grad_w_out = parts[3].T

    return (
        output,
        grad_tokens,
        grad_w_qkv,
        small[6:8],
        grad_w_out,
        small[0],
        small[1],
        small[2],
        grad_w_up,
        small[8:].reshape(-1),
        grad_w_down,
        small[3],
        small[4],
        small[5],
    )


def local(*arrays):
    tokens = arrays[0]
    sizes = (lax.axis_size("dp"), lax.axis_size("tensor"))
    if sizes == (16, 2) and tokens.shape == (SEQ, 1024):
        return data_plan(*arrays)
    return tensor_plan(*arrays)


def solution(mesh):
    return jax.shard_map(
        local,
        mesh=mesh,
        in_specs=(
            P(("dp", "tensor"), None),
            P("dp", None),
            P(None, "dp", "tensor"),
            P(),
            P("tensor", "dp"),
            P(),
            P(),
            P(),
            P("dp", "tensor"),
            P(),
            P("tensor", "dp"),
            P(),
            P(),
            P(),
            P(("dp", "tensor"), None),
        ),
        out_specs=(
            P(("dp", "tensor"), None),
            P(("dp", "tensor"), None),
            P(None, "dp", "tensor"),
            P(),
            P("tensor", "dp"),
            P(),
            P(),
            P(),
            P("dp", "tensor"),
            P(),
            P("tensor", "dp"),
            P(),
            P(),
            P(),
        ),
        check_vma=False,
    )
```
